256 devices in a mesh: attn: 16 (over z, y_lo), exp: 16 (over x, y_hi, core).
Axes of the slice: x: 4, y: 4 (y_hi: 2, y_lo: 2; y = y_hi * 2 + y_lo), z: 8, core: 2. Of those that a mesh axis runs over, the one named last changes fastest.
Arguments:
- hidden_rows: bfloat16 [4096, 2880], P('attn'), may hold values from -6 to 6
- attention_gain: float32 [2880], replicated, may hold values from 0.1 to 1.9
- input_weight: bfloat16 [2880, 2560], P(None, 'exp'), may hold values from -0.109375 to 0.109375
- cache_keys: bfloat16 [4096, 128, 256], P(('attn', 'exp')), may hold values from -128 to 128
- cache_values: bfloat16 [4096, 128, 256], P(('attn', 'exp')), may hold values from -6 to 6
- context_length: int32 [4096], P(('attn', 'exp')), may hold values from 1 to 255
- sink_logits: float32 [32], replicated, may hold values from 2 to 7
- out_weight: bfloat16 [2048, 2880], P('exp'), may hold values from -0.125 to 0.125
- expert_gain: float32 [2880], replicated, may hold values from 0.1 to 1.9
- expert_index: int32 [4096, 4], P(('attn', 'exp')), may hold values from 0 to 63, all different within a row; in each aligned block of 16 rows (0 to 15, 16 to 31, ...) at most 2 rows name the same one
- expert_share: float32 [4096, 4], P(('attn', 'exp')), may hold values from 0.05 to 1
- gate_weight: bfloat16 [92160, 2880], P(('attn', 'exp')), may hold values from -0.109375 to 0.109375
- up_weight: bfloat16 [92160, 2880], P(('attn', 'exp')), may hold values from -0.109375 to 0.109375
- down_weight: bfloat16 [92160, 2880], P(('attn', 'exp')), may hold values from -0.15625 to 0.15625
Outputs:
- layer_out: bfloat16 [4096, 2880], P(('attn', 'exp'))
The draws below stay inside these ranges and needn't reach their ends.
Inputs may be any that keep to these rules, and one draw needn't show every extreme that they name: `expert_index`: A row names 4 different experts. In each aligned block of 16 rows no expert is named more than 2 times, a bound that some block reaches.
All inputs are finite; a program needn't handle non-finite values.
Results may differ from the reference program's by a relative error of at most 0.019.
Values may be sent and summed in bfloat16 or wider, within the bound.
A program may use at most 64 MiB of HBM per device.

```python
import math
import jax
import jax.numpy as jnp
import numpy as np
from jax import lax

D = 2880
FF = 1440
HEAD = 64
QHEADS = 32
KVHEADS = 4
WINDOW = 128
TOPK = 4
CAP = 2
TOK_DEV = 16
EXPERTS = 64
QUARTERS = 4
ROWS = 4096
N_ATTN = 16
N_EXP = 16


def draw_cache_keys(key, part):
    key = jax.random.fold_in(key, 7)
    values = 2.0 * jax.random.normal(key, (ROWS, WINDOW, KVHEADS * HEAD), jnp.float32)
    return jnp.clip(values, -12.0, 12.0).astype(jnp.bfloat16)


def place_ends(values, key, low, largest):
    longest = values.shape.index(max(values.shape))
    spots = []
    for shift in (0, 1):
        where = [jax.random.randint(jax.random.fold_in(key, axis), (), 0, length) for axis, length in enumerate(values.shape)]
        where[longest] = (where[longest] + shift) % values.shape[longest]
        spots.append(tuple(where))
    return values.at[spots[0]].set(low).at[spots[1]].set(largest)


def block_levels(stream_key, dims, split, least, top_value):
    loudness, own = 1.0, jax.random.fold_in(stream_key, 6)
    for dim, shards_of in split:
        steps = jnp.exp(jax.random.uniform(jax.random.fold_in(own, dim), (shards_of,), jnp.float32, least / len(split), top_value / len(split)))
        loudness = loudness * jnp.repeat(steps, dims[dim] // shards_of).reshape([-1 if axis == dim else 1 for axis in range(len(dims))])
    return loudness


def assign_block(stream_key, own, number, rows, count, top, reach, skew):
    order = jax.random.permutation(stream_key, count)
    crowded, usual = portions_of(count, rows * top, reach, skew, True), portions_of(count, rows * top, reach, skew, False)
    places = jnp.arange(count)

    def named(sizes, offset_by):
        used = int((sizes > 0).sum())
        fixed = max(1, used // 4)
        shifted = fixed + (places - fixed + offset_by * (used - fixed)) % max(1, count - fixed)
        return jnp.zeros((count,), jnp.int32).at[order[jnp.where(places < fixed, places, shifted)]].set(jnp.asarray(sizes, jnp.int32))

    sizes = jnp.where(number % 4 == 0, named(crowded, number // 4), named(usual, number - number // 4 - 1))
    mixed = jax.random.permutation(jax.random.fold_in(own, 3), count)
    giver, taker = mixed[0:count // 2 * 2:2], mixed[1:count // 2 * 2:2]
    slack = jnp.minimum(sizes[giver] - 1, reach - sizes[taker]) // 2
    slack = jnp.where((giver == order[0]) | (taker == order[0]) | (sizes[taker] == 0), 0, jnp.maximum(slack, 0))
    shifted = jax.random.randint(jax.random.fold_in(own, 4), (count // 2,), 0, 1 << 20) % (slack + 1)
    sizes = sizes.at[giver].add(-shifted).at[taker].add(shifted)
    members = jnp.searchsorted(jnp.cumsum(sizes), jnp.arange(rows * top), side="right").astype(jnp.int32)
    listing = members.reshape(top, rows).T
    listing = listing[jax.random.permutation(jax.random.fold_in(own, 1), rows)]
    offset_by = jax.random.randint(jax.random.fold_in(own, 2), (rows, 1), 0, top)
    return jnp.take_along_axis(listing, (jnp.arange(top)[None, :] + offset_by) % top, axis=1)


def portions_of(number_of, total, most, slope, full):
    portions = [(1 << 20) // math.isqrt(grade ** slope) + 1 for grade in range(1, number_of + 1)]
    largest = most if full else min(most, max(-(-total // number_of), total * portions[0] // sum(portions)))
    least = 1 if total - largest >= number_of - 1 else 0
    holding, rest = [largest] + [least] * (number_of - 1), total - largest - least * (number_of - 1)
    while rest > 0:
        candidates = [i for i in range(1, number_of) if holding[i] < largest] or [i for i in range(1, number_of) if holding[i] < most]
        mass, left = sum([portions[i] for i in candidates]), rest
        for i in candidates:
            extra = min(most - holding[i], max(1, left * portions[i] // mass), rest)
            holding[i] = holding[i] + extra
            rest = rest - extra
    return np.array(holding)


def bell_draw(stream_key, shape, spread, most, split=(), kind=jnp.bfloat16):
    entries = spread * jax.random.normal(stream_key, shape, jnp.float32)
    if split:
        entries = entries * block_levels(stream_key, shape, split, -0.22, 0.18)
    return jnp.clip(entries, -most, most).astype(kind)


def setup_inputs(seed: int = 0) -> dict:
    seeds = jax.random.split(jax.random.key(seed), 15)
    hidden_rows = bell_draw(seeds[0], (ROWS, D), 1.0, 6.0, ((0, 16),))
    attention_gain = jnp.clip(1.0 + 0.18 * jax.random.normal(seeds[1], (D,), jnp.float32), 0.1, 1.9)
    input_weight = bell_draw(seeds[2], (D, (QHEADS + 2 * KVHEADS) * HEAD), D ** -0.5, 0.109375, ((1, 16),))
    cache_keys = draw_cache_keys(jax.random.fold_in(seeds[14], 71), 0)
    cache_values = bell_draw(seeds[4], (ROWS, WINDOW, KVHEADS * HEAD), 1.0, 6.0, ((0, 256),))
    context_length = place_ends(jax.random.randint(seeds[5], (ROWS,), 1, 2 * WINDOW), jax.random.fold_in(seeds[5], 1), 1, (2 * WINDOW) - 1).astype(jnp.int32)
    sink_logits = jnp.clip(jax.random.uniform(seeds[6], (QHEADS,), jnp.float32, 2.0, 7.0), 2.0, 7.0)
    out_weight = bell_draw(seeds[7], (QHEADS * HEAD, D), (QHEADS * HEAD) ** -0.5, 0.125, ((0, 16),))
    expert_gain = jnp.clip(1.0 + 0.18 * jax.random.normal(seeds[8], (D,), jnp.float32), 0.1, 1.9)
    expert_index_keys = jax.random.split(jax.random.fold_in(seeds[9], 1), ROWS // TOK_DEV)
    expert_index_turns = jax.random.permutation(jax.random.fold_in(seeds[9], 3), ROWS // TOK_DEV)
    expert_index = jax.vmap(lambda own, number: assign_block(jax.random.fold_in(seeds[9], 2), own, number, TOK_DEV, EXPERTS, TOPK, CAP, 2))(expert_index_keys, expert_index_turns).reshape((ROWS, TOPK))
    expert_share = jnp.clip(0.05 + 0.95 * jax.random.uniform(seeds[10], (ROWS, TOPK), jnp.float32) ** block_levels(seeds[10], (ROWS, TOPK), ((0, 256),), -0.2, 0.2), 0.05, 1.0)
    gate_weight = bell_draw(seeds[11], (EXPERTS * FF, D), D ** -0.5, 0.109375, ((0, 256),))
    up_weight = bell_draw(seeds[12], (EXPERTS * FF, D), D ** -0.5, 0.109375, ((0, 256),))
    down_weight = bell_draw(seeds[13], (EXPERTS * FF, D), FF ** -0.5, 0.15625, ((0, 256),))
    return dict(hidden_rows=hidden_rows, attention_gain=attention_gain, input_weight=input_weight, cache_keys=cache_keys, cache_values=cache_values, context_length=context_length, sink_logits=sink_logits, out_weight=out_weight, expert_gain=expert_gain, expert_index=expert_index, expert_share=expert_share, gate_weight=gate_weight, up_weight=up_weight, down_weight=down_weight)


def normed(values, gain_vec):
    widened = values.astype(jnp.float32)
    return widened * lax.rsqrt(lax.optimization_barrier(jnp.mean(widened * widened, axis=-1, keepdims=True)) + 1e-05) * gain_vec.astype(jnp.float32)

def rotated(blocks, positions):
    half_dim = blocks.shape[-1] // 2
    frequency = 150000.0 ** (-jnp.arange(half_dim, dtype=jnp.float32) / half_dim)
    angles = positions.astype(jnp.float32)[:, None, None] * frequency
    cosine = jnp.cos(angles)
    sine_part = jnp.sin(angles)
    first_half = blocks[..., :half_dim]
    second_half = blocks[..., half_dim:]
    return jnp.concatenate([first_half * cosine - second_half * sine_part, second_half * cosine + first_half * sine_part], axis=-1)

def reference(hidden_rows, attention_gain, input_weight, cache_keys, cache_values, context_length, sink_logits, out_weight, expert_gain, expert_index, expert_share, gate_weight, up_weight, down_weight):
    group_size = QHEADS // KVHEADS
    query_width = QHEADS * HEAD
    key_width = KVHEADS * HEAD
    score_scale = HEAD ** (-0.5)
    normed_in = normed(hidden_rows, attention_gain).astype(jnp.bfloat16)
    projections = jnp.dot(normed_in, input_weight, preferred_element_type=jnp.float32).astype(jnp.bfloat16)
    projections = lax.optimization_barrier(projections).astype(jnp.float32)
    queries = rotated(projections[:, :query_width].reshape(ROWS, QHEADS, HEAD), context_length)
    new_keys = rotated(projections[:, query_width:query_width + key_width].reshape(ROWS, KVHEADS, HEAD), context_length)
    new_values = projections[:, query_width + key_width:].reshape(ROWS, KVHEADS, HEAD)
    group_rows = ROWS // N_ATTN

    def attend(pieces):
        query_part, key_part, value_part, cached_keys, cached_values, length_part = pieces
        row_count = query_part.shape[0]
        query_heads = query_part.reshape(row_count, KVHEADS, group_size, HEAD)
        key_heads = cached_keys.astype(jnp.float32).reshape(row_count, WINDOW, KVHEADS, HEAD)
        value_heads = cached_values.astype(jnp.float32).reshape(row_count, WINDOW, KVHEADS, HEAD)
        scores = jnp.einsum('rkgd,rwkd->rkgw', query_heads, key_heads) * score_scale
        slot_index = jnp.arange(WINDOW, dtype=jnp.int32)
        valid_mask = (slot_index[None, :] >= WINDOW - length_part[:, None])[:, None, None, :]
        own_score = jnp.einsum('rkgd,rkd->rkg', query_heads, key_part) * score_scale
        sink_part = sink_logits.astype(jnp.float32).reshape(1, KVHEADS, group_size)
        highest = jnp.maximum(lax.optimization_barrier(jnp.max(jnp.where(valid_mask, scores, -1e+30), axis=-1)), jnp.maximum(own_score, sink_part))
        weights = jnp.where(valid_mask, jnp.exp(scores - highest[..., None]), 0.0)
        own_weight = jnp.exp(own_score - highest)
        denominator = lax.optimization_barrier(jnp.sum(weights, axis=-1)) + own_weight + jnp.exp(sink_part - highest)
        mixed_rows = jnp.einsum('rkgw,rwkd->rkgd', weights, value_heads) + own_weight[..., None] * value_part[:, :, None, :]
        return (mixed_rows / denominator[..., None]).reshape(row_count, query_width).astype(jnp.bfloat16)
    attended = lax.map(attend, (queries.reshape(N_ATTN, group_rows, QHEADS, HEAD), new_keys.reshape(N_ATTN, group_rows, KVHEADS, HEAD), new_values.reshape(N_ATTN, group_rows, KVHEADS, HEAD), cache_keys.reshape(N_ATTN, group_rows, WINDOW, key_width), cache_values.reshape(N_ATTN, group_rows, WINDOW, key_width), context_length.reshape(N_ATTN, group_rows))).reshape(ROWS, query_width)
    residual = hidden_rows.astype(jnp.float32) + jnp.dot(attended, out_weight, preferred_element_type=jnp.float32)
    expert_in = normed(residual, expert_gain).astype(jnp.bfloat16)
    device_total = N_ATTN * N_EXP
    pair_count = TOK_DEV * TOPK
    pair_ids = expert_index.reshape(device_total, pair_count)
    onehot = (pair_ids[:, :, None] == jnp.arange(EXPERTS, dtype=jnp.int32)[None, None, :]).astype(jnp.int32)
    earlier = jnp.cumsum(onehot, axis=1, dtype=jnp.int32) - onehot
    slot_of = lax.optimization_barrier(jnp.sum(earlier * onehot, axis=-1, dtype=jnp.int32))
    device_of = jnp.broadcast_to(jnp.arange(device_total, dtype=jnp.int32)[:, None], (device_total, pair_count))
    row_of = device_of * TOK_DEV + jnp.arange(pair_count, dtype=jnp.int32)[None, :] // TOPK
    table = jnp.full((EXPERTS, device_total, CAP), ROWS, jnp.int32).at[pair_ids, device_of, slot_of].set(row_of)
    padded = jnp.concatenate([expert_in, jnp.zeros((1, D), jnp.bfloat16)], axis=0)
    part_width = FF // QUARTERS
    contract = (((1,), (1,)), ((), ()))

    def expert(pieces):
        index_rows, gate_rows, up_rows, down_rows = pieces
        inputs = padded[index_rows.reshape(-1)]
        gate_out = lax.dot_general(inputs, gate_rows, contract, preferred_element_type=jnp.float32)
        up_out = lax.dot_general(inputs, up_rows, contract, preferred_element_type=jnp.float32)
        active = (jax.nn.silu(gate_out) * up_out).astype(jnp.bfloat16)
        summed = jnp.zeros((inputs.shape[0], D), jnp.float32)
        for quarter in range(QUARTERS):
            piece = jnp.dot(active[:, quarter * part_width:(quarter + 1) * part_width], down_rows[quarter * part_width:(quarter + 1) * part_width], preferred_element_type=jnp.float32).astype(jnp.bfloat16)
            summed = summed + lax.optimization_barrier(piece).astype(jnp.float32)
        return summed.astype(jnp.bfloat16)
    expert_out = lax.map(expert, (table, gate_weight.reshape(EXPERTS, FF, D), up_weight.reshape(EXPERTS, FF, D), down_weight.reshape(EXPERTS, FF, D)))
    expert_out = lax.optimization_barrier(expert_out).reshape(EXPERTS * device_total * CAP, D)
    flat_index = pair_ids * (device_total * CAP) + device_of * CAP + slot_of
    picked = expert_out[flat_index.reshape(-1)].astype(jnp.float32)
    weighted = (picked * expert_share.reshape(-1)[:, None]).reshape(ROWS, TOPK, D)
    return (residual + lax.optimization_barrier(jnp.sum(weighted, axis=1))).astype(jnp.bfloat16)
```

```python
import jax
import jax.numpy as jnp
from jax import lax
from jax.experimental import pallas as pl
from jax.experimental.pallas import tpu as pltpu
from jax.sharding import PartitionSpec as P

HEAD = 64
QHEADS = 32
KVHEADS = 4
TOK_DEV = 16


def normed(values, gain_vec):
    widened = values.astype(jnp.float32)
    return (
        widened * lax.rsqrt(jnp.mean(widened * widened, axis=-1, keepdims=True) + 1e-05) * gain_vec
    )


def rotated(blocks, positions):
    half_dim = blocks.shape[-1] // 2
    frequency = 150000.0 ** (-jnp.arange(half_dim, dtype=jnp.float32) / half_dim)
    angles = positions.astype(jnp.float32)[:, None, None] * frequency
    cosine = jnp.cos(angles)
    sine_part = jnp.sin(angles)
    first_half = blocks[..., :half_dim]
    second_half = blocks[..., half_dim:]
    return jnp.concatenate(
        [
            first_half * cosine - second_half * sine_part,
            second_half * cosine + first_half * sine_part,
        ],
        axis=-1,
    )


D = 2880
FFQ = 360
CHUNKS = ((0, 768), (768, 768), (1536, 768), (2304, 576))
NC = len(CHUNKS)
BF = jnp.bfloat16
F32 = jnp.float32
MESH = pl.DeviceIdType.MESH
NT = (((1,), (1,)), ((), ()))


def place():
    attn = lax.axis_index("attn")
    exp = lax.axis_index("exp")
    return dict(
        attn=attn,
        exp=exp,
        z=lax.div(attn, 2),
        y_lo=lax.rem(attn, 2),
        x=lax.div(exp, 4),
        y_hi=lax.rem(lax.div(exp, 2), 2),
        core=lax.rem(exp, 2),
    )


def z_peer(me, d):
    other = lax.rem(me["z"] + d, 8)
    return other, (other * 2 + me["y_lo"], me["exp"])


def plane_peer(me, d):
    other = lax.rem(me["q"] + d, 16)
    y_hi, y_lo, x = lax.div(other, 8), lax.rem(lax.div(other, 4), 2), lax.rem(other, 4)
    return other, (me["z"] * 2 + y_lo, (x * 2 + y_hi) * 2 + me["core"])


def group_peer(me, d):
    other = lax.rem(me["g"] + d, 8)
    return other, (me["attn"], other * 2 + me["core"])


def remote(src, dst, send_sem, recv_sem, device):
    return pltpu.make_async_remote_copy(
        src_ref=src,
        dst_ref=dst,
        send_sem=send_sem,
        recv_sem=recv_sem,
        device_id=device,
        device_id_type=MESH,
    )


def wait_bytes(ref, sem):
    pltpu.make_async_copy(ref, ref, sem).wait()


def spread(count, peer, me, src, dst, own, send_sem, recv_sem):
    @pl.loop(1, count)
    def _(d):
        other, device = peer(me, d)
        remote(src.at[other], dst.at[own], send_sem, recv_sem, device).start()


def layer_tail(
    att,
    w_out,
    hidden,
    gain,
    index,
    share,
    gate_hbm,
    up_hbm,
    down_hbm,
    out,
    *scratch,
):
    s = dict(zip(SCRATCH_NAMES, scratch))
    part = {
        name: [s[f"{name}{c}"] for c in range(NC)] for name in CHUNKED
    }
    me = place()
    me["q"] = me["y_hi"] * 8 + me["y_lo"] * 4 + me["x"]
    me["g"] = me["x"] * 2 + me["y_hi"]
    core, partner = me["core"], (me["attn"], me["exp"] + 1 - 2 * me["core"])

    loads = [
        pltpu.make_async_copy(gate_hbm, s["gate"], s["load_sem"].at[0]),
        pltpu.make_async_copy(up_hbm, s["up"], s["load_sem"].at[1]),
        pltpu.make_async_copy(down_hbm, s["down"], s["load_sem"].at[2]),
    ]
    for load in loads:
        load.start()

    barrier = pltpu.get_barrier_semaphore()

    @pl.loop(1, 8)
    def _(d):
        pl.semaphore_signal(barrier, inc=1, device_id=z_peer(me, d)[1], device_id_type=MESH)

    @pl.loop(1, 16)
    def _(d):
        pl.semaphore_signal(barrier, inc=1, device_id=plane_peer(me, d)[1], device_id_type=MESH)

    pl.semaphore_signal(barrier, inc=1, device_id=partner, device_id_type=MESH)
    pl.semaphore_wait(barrier, 23)

    core_copies = []
    att_mine = att[:, pl.ds(core, 1)].reshape(128, 128)
    att_other = att[:, pl.ds(1 - core, 1)].reshape(128, 128)
    for c, (c0, width) in enumerate(CHUNKS):
        columns = w_out[:, c0 : c0 + width]
        part["rcs"][c][...] = jnp.dot(att_other, columns, preferred_element_type=F32).astype(BF)
        copy = remote(
            part["rcs"][c], part["rcr"][c], s["rc_send"].at[c], s["rc_recv"].at[c], partner
        )
        copy.start()
        core_copies.append(copy)
        part["rmine"][c][...] = jnp.dot(att_mine, columns, preferred_element_type=F32)
    for c, (c0, width) in enumerate(CHUNKS):
        core_copies[c].wait_recv()
        total = part["rmine"][c][...] + part["rcr"][c][...].astype(F32)
        part["rsum"][c][...] = total.astype(BF).reshape(8, 16, width)
        spread(
            8, group_peer, me, part["rsum"][c], part["rrec"][c], me["g"],
            s["rs_send"].at[c], s["rs_recv"].at[c],
        )
        part["rrec"][c][me["g"]] = part["rsum"][c][me["g"]]

    slot_lane = lax.broadcasted_iota(jnp.int32, (16, 128), 1)
    expert_lane = lax.div(slot_lane, 2)
    named = jnp.zeros((16, 128), F32)
    weight = jnp.zeros((16, 128), F32)
    for k in range(4):
        hit = index[:, k : k + 1] == expert_lane
        named = named + jnp.where(hit, 1.0, 0.0)
        weight = weight + jnp.where(hit, share[:, k : k + 1], 0.0)
    row = lax.broadcasted_iota(jnp.int32, (16, 16), 0)
    column = lax.broadcasted_iota(jnp.int32, (16, 16), 1)
    before = jnp.where(column < row, 1.0, 0.0).astype(BF)
    earlier = jnp.dot(before, named.astype(BF), preferred_element_type=F32)
    taken = jnp.where(earlier == lax.rem(slot_lane, 2).astype(F32), named, 0.0)
    weight = weight * taken
    weight_hi = weight.astype(BF)
    weight_lo = (weight - weight_hi.astype(F32)).astype(BF)
    wide_row = lax.broadcasted_iota(jnp.int32, (128, 128), 0)
    wide_column = lax.broadcasted_iota(jnp.int32, (128, 128), 1)
    identity = jnp.where(wide_row == wide_column, 1.0, 0.0).astype(BF)
    placing = lax.dot_general(identity, taken.astype(BF), NT, preferred_element_type=F32).astype(BF)
    by_expert = lax.rem(lax.div(wide_row, 2), 8) * 16 + lax.div(wide_row, 16) * 2 + lax.rem(wide_row, 2)
    to_expert = jnp.where(by_expert == wide_column, 1.0, 0.0).astype(BF)

    square_sum = jnp.zeros((16, 1), F32)
    for c, (c0, width) in enumerate(CHUNKS):
        wait_bytes(part["rrec"][c].at[0:7], s["rs_recv"].at[c])
        residual = hidden[:, c0 : c0 + width].astype(F32) + jnp.sum(
            part["rrec"][c][...].astype(F32), axis=0
        )
        s["residual"][:, c0 : c0 + width] = residual
        square_sum = square_sum + jnp.sum(residual * residual, axis=1, keepdims=True)
    scale = lax.rsqrt(square_sum / D + 1e-05)

    for c, (c0, width) in enumerate(CHUNKS):
        expert_in = (
            s["residual"][:, c0 : c0 + width] * scale * gain[:, c0 : c0 + width]
        ).astype(BF)
        placed = jnp.dot(placing, expert_in, preferred_element_type=F32).astype(BF)
        part["zs"][c][...] = placed.reshape(8, 16, width)
        spread(
            8, z_peer, me, part["zs"][c], part["zr"][c], me["z"],
            s["z_send"].at[c], s["z_recv"].at[c],
        )
        part["zr"][c][me["z"]] = part["zs"][c][me["z"]]

    def plane_out(c):
        width = CHUNKS[c][1]
        wait_bytes(part["zr"][c].at[0:7], s["z_recv"].at[c])
        rows = part["zr"][c][...].reshape(128, width)
        part["ps"][c][...] = (
            jnp.dot(to_expert, rows, preferred_element_type=F32).astype(BF).reshape(8, 16, width)
        )

        @pl.loop(1, 16)
        def _(d):
            other, device = plane_peer(me, d)
            remote(
                part["ps"][c].at[lax.rem(other, 8)],
                part["xin"][c].at[core, me["q"]],
                s["p_send"].at[c],
                s["p_recv"].at[c],
                device,
            ).start()

        part["xin"][c][core, me["q"]] = part["ps"][c][lax.rem(me["q"], 8)]

    swap_copies = {}

    def swap_out(c):
        mine = part["xin"][c].at[core]
        wait_bytes(part["xin"][c].at[0, 0:15], s["p_recv"].at[c])
        swap_copies[c] = remote(mine, mine, s["x_send"].at[c], s["x_recv"].at[c], partner)
        swap_copies[c].start()

    def hidden_units(c):
        c0, width = CHUNKS[c]
        swap_copies[c].wait_recv()
        if c == 0:
            loads[0].wait()
            loads[1].wait()
        rows = part["xin"][c][...].reshape(512, width)
        for weights, total in (("gate", "gate_out"), ("up", "up_out")):
            product = lax.dot_general(
                rows, s[weights][:, c0 : c0 + width], NT, preferred_element_type=F32
            )
            if c == 0:
                s[total][...] = product
            else:
                s[total][...] += product

    for step in range(NC + 2):
        if step < NC:
            plane_out(step)
        if 0 <= step - 1 < NC:
            swap_out(step - 1)
        if 0 <= step - 2 < NC:
            hidden_units(step - 2)

    gate_out = s["gate_out"][...]
    s["active"][...] = (gate_out / (1.0 + jnp.exp(-gate_out)) * s["up_out"][...]).astype(BF)
    loads[2].wait()

    back_copies = []
    for c, (c0, width) in enumerate(CHUNKS):
        columns = s["down"][:, c0 : c0 + width]
        other_rows = s["active"][pl.ds(pl.multiple_of((1 - core) * 256, 256), 256), :]
        part["ycs"][c][...] = jnp.dot(other_rows, columns, preferred_element_type=F32).astype(BF)
        copy = remote(
            part["ycs"][c], part["ycr"][c], s["y_send"].at[c], s["y_recv"].at[c], partner
        )
        copy.start()
        back_copies.append(copy)
        my_rows = s["active"][pl.ds(pl.multiple_of(core * 256, 256), 256), :]
        part["ymine"][c][...] = jnp.dot(my_rows, columns, preferred_element_type=F32)

    def plane_back(c):
        width = CHUNKS[c][1]
        back_copies[c].wait_recv()
        total = part["ymine"][c][...] + part["ycr"][c][...].astype(F32)
        part["ysum"][c][...] = total.astype(BF).reshape(16, 16, width)
        spread(
            16, plane_peer, me, part["ysum"][c], part["pr"][c], me["q"],
            s["b_send"].at[c], s["b_recv"].at[c],
        )
        part["pr"][c][me["q"]] = part["ysum"][c][me["q"]]

    back_row = lax.broadcasted_iota(jnp.int32, (128, 256), 0)
    back_column = lax.broadcasted_iota(jnp.int32, (128, 256), 1)
    by_source = (
        lax.rem(lax.div(back_row, 2), 8) * 16 + lax.div(back_row, 16) * 2 + lax.rem(back_row, 2)
    )
    to_source = jnp.where(by_source == lax.rem(back_column, 128), 1.0, 0.0).astype(BF)

    def z_back(c):
        width = CHUNKS[c][1]
        wait_bytes(part["pr"][c].at[0:15], s["b_recv"].at[c])
        rows = part["pr"][c][...].reshape(256, width)
        part["vs"][c][...] = (
            jnp.dot(to_source, rows, preferred_element_type=F32).astype(BF).reshape(8, 16, width)
        )
        spread(
            8, z_peer, me, part["vs"][c], part["vr"][c], me["z"],
            s["v_send"].at[c], s["v_recv"].at[c],
        )
        part["vr"][c][me["z"]] = part["vs"][c][me["z"]]

    def finish(c):
        c0, width = CHUNKS[c]
        wait_bytes(part["vr"][c].at[0:7], s["v_recv"].at[c])
        rows = part["vr"][c][...].reshape(128, width)
        mixed = jnp.dot(weight_hi, rows, preferred_element_type=F32) + jnp.dot(
            weight_lo, rows, preferred_element_type=F32
        )
        out[:, c0 : c0 + width] = (s["residual"][:, c0 : c0 + width] + mixed).astype(BF)

    for step in range(NC + 2):
        if step < NC:
            plane_back(step)
        if 0 <= step - 1 < NC:
            z_back(step - 1)
        if 0 <= step - 2 < NC:
            finish(step - 2)

    for c in range(NC):
        core_copies[c].wait_send()
        swap_copies[c].wait_send()
        back_copies[c].wait_send()
        wait_bytes(part["rsum"][c].at[0:7], s["rs_send"].at[c])
        wait_bytes(part["zs"][c].at[0:7], s["z_send"].at[c])
        wait_bytes(part["xin"][c].at[0, 0:15], s["p_send"].at[c])
        wait_bytes(part["ysum"][c].at[0:15], s["b_send"].at[c])
        wait_bytes(part["vs"][c].at[0:7], s["v_send"].at[c])


CHUNKED = {
    "rcs": ((128,), BF),
    "rcr": ((128,), BF),
    "rmine": ((128,), F32),
    "rsum": ((8, 16), BF),
    "rrec": ((8, 16), BF),
    "zs": ((8, 16), BF),
    "zr": ((8, 16), BF),
    "ps": ((8, 16), BF),
    "xin": ((2, 16, 16), BF),
    "ycs": ((256,), BF),
    "ycr": ((256,), BF),
    "ymine": ((256,), F32),
    "ysum": ((16, 16), BF),
    "pr": ((16, 16), BF),
    "vs": ((8, 16), BF),
    "vr": ((8, 16), BF),
}
SCRATCH = {
    f"{name}{c}": pltpu.VMEM((*lead, CHUNKS[c][1]), dtype)
    for name, (lead, dtype) in CHUNKED.items()
    for c in range(NC)
}
SCRATCH["gate"] = pltpu.VMEM((FFQ, D), BF)
SCRATCH["up"] = pltpu.VMEM((FFQ, D), BF)
SCRATCH["down"] = pltpu.VMEM((FFQ, D), BF)
SCRATCH["residual"] = pltpu.VMEM((16, D), F32)
SCRATCH["gate_out"] = pltpu.VMEM((512, FFQ), F32)
SCRATCH["up_out"] = pltpu.VMEM((512, FFQ), F32)
SCRATCH["active"] = pltpu.VMEM((512, FFQ), BF)
SCRATCH["load_sem"] = pltpu.SemaphoreType.DMA((3,))
for way in ("rc", "rs", "z", "p", "x", "y", "b", "v"):
    SCRATCH[f"{way}_send"] = pltpu.SemaphoreType.DMA((NC,))
    SCRATCH[f"{way}_recv"] = pltpu.SemaphoreType.DMA((NC,))
SCRATCH_NAMES = tuple(SCRATCH)


def run_tail(att, w_out, hidden, gain, index, share, gate, up, down):
    vmem = pl.BlockSpec(memory_space=pltpu.VMEM)
    anywhere = pl.BlockSpec(memory_space=pl.ANY)
    return pl.pallas_call(
        layer_tail,
        out_shape=jax.ShapeDtypeStruct((16, D), BF),
        in_specs=[vmem] * 6 + [anywhere] * 3,
        out_specs=vmem,
        scratch_shapes=list(SCRATCH.values()),
        compiler_params=pltpu.CompilerParams(
            collective_id=0, has_side_effects=True, vmem_limit_bytes=58 * 1024 * 1024
        ),
        cost_estimate=pl.CostEstimate(
            flops=3_600_000_000, bytes_accessed=8_000_000, transcendentals=200_000
        ),
        name="layer_tail",
    )(att, w_out, hidden, gain, index, share, gate, up, down)


def per_device(
    hidden_rows,
    attention_gain,
    input_weight,
    cache_keys,
    cache_values,
    context_length,
    sink_logits,
    out_weight,
    expert_gain,
    expert_index,
    expert_share,
    gate_weight,
    up_weight,
    down_weight,
):
    exp_index = lax.axis_index("exp")
    group_size = QHEADS // KVHEADS
    query_width = QHEADS * HEAD
    key_width = KVHEADS * HEAD
    score_scale = HEAD ** (-0.5)
    window_len = cache_keys.shape[1]
    normed_in = normed(hidden_rows, attention_gain).astype(jnp.bfloat16)
    projected = jnp.dot(normed_in, input_weight, preferred_element_type=jnp.float32).astype(
        jnp.bfloat16
    )
    own_proj = lax.all_to_all(projected, "exp", split_axis=0, concat_axis=1, tiled=True).astype(
        jnp.float32
    )
    row_count = own_proj.shape[0]
    queries = rotated(own_proj[:, :query_width].reshape(row_count, QHEADS, HEAD), context_length)
    new_keys = rotated(
        own_proj[:, query_width : query_width + key_width].reshape(row_count, KVHEADS, HEAD),
        context_length,
    )
    new_values = own_proj[:, query_width + key_width :].reshape(row_count, KVHEADS, HEAD)
    query_heads = queries.reshape(row_count, KVHEADS, group_size, HEAD)
    key_heads = cache_keys.astype(jnp.float32).reshape(row_count, window_len, KVHEADS, HEAD)
    value_heads = cache_values.astype(jnp.float32).reshape(row_count, window_len, KVHEADS, HEAD)
    scores = jnp.einsum("rkgd,rwkd->rkgw", query_heads, key_heads) * score_scale
    slot_index = jnp.arange(window_len, dtype=jnp.int32)
    valid_mask = (slot_index[None, :] >= window_len - context_length[:, None])[:, None, None, :]
    own_score = jnp.einsum("rkgd,rkd->rkg", query_heads, new_keys) * score_scale
    sink_part = sink_logits.reshape(1, KVHEADS, group_size)
    highest = jnp.maximum(
        jnp.max(jnp.where(valid_mask, scores, -1e30), axis=-1), jnp.maximum(own_score, sink_part)
    )
    weights = jnp.where(valid_mask, jnp.exp(scores - highest[..., None]), 0.0)
    own_weight = jnp.exp(own_score - highest)
    denominator = jnp.sum(weights, axis=-1) + own_weight + jnp.exp(sink_part - highest)
    mixed_rows = (
        jnp.einsum("rkgw,rwkd->rkgd", weights, value_heads)
        + own_weight[..., None] * new_values[:, :, None, :]
    )
    attended_own = (
        (mixed_rows / denominator[..., None]).reshape(row_count, query_width).astype(jnp.bfloat16)
    )
    attended = lax.all_to_all(attended_own, "exp", split_axis=1, concat_axis=0, tiled=True)
    hidden_own = lax.dynamic_slice_in_dim(hidden_rows, exp_index * TOK_DEV, TOK_DEV, 0)
    return run_tail(
        attended.reshape(8, 2, TOK_DEV, 128),
        out_weight,
        hidden_own,
        expert_gain[None, :],
        expert_index,
        expert_share,
        gate_weight,
        up_weight,
        down_weight,
    )


def solution(mesh):
    return jax.shard_map(
        per_device,
        mesh=mesh,
        in_specs=(
            P("attn", None),
            P(),
            P(None, "exp"),
            P(("attn", "exp"), None, None),
            P(("attn", "exp"), None, None),
            P(("attn", "exp")),
            P(),
            P("exp", None),
            P(),
            P(("attn", "exp"), None),
            P(("attn", "exp"), None),
            P(("attn", "exp"), None),
            P(("attn", "exp"), None),
            P(("attn", "exp"), None),
        ),
        out_specs=P(("attn", "exp"), None),
        check_vma=False,
    )
```

```python
import math
from types import SimpleNamespace

import jax
import jax.numpy as jnp
from jax import lax
from jax.experimental import pallas as pl
from jax.experimental.pallas import tpu as pltpu
from jax.sharding import PartitionSpec as P

D = 2880
FFQ = 360
CHUNKS = ((0, 512), (512, 512), (1024, 512), (1536, 512), (2048, 512), (2560, 320))
NC = len(CHUNKS)
DISPATCH_TIMES = ((0, 1), (2.1, 1), (4.2, 1), (6.3, 1), (7.4, 1))
RETURN_TIMES = ((0, 1), (1.1, 1), (4.2, 1), (7.3, 1))
WIDTHS = tuple((width + 127) // 128 * 128 for _, width in CHUNKS) + (128,)
BF = jnp.bfloat16
F32 = jnp.float32
MESH = pl.DeviceIdType.MESH
NT = (((1,), (1,)), ((), ()))
PA, AA, RC, RS, Z, PLANE, SWAP, BC, BP, BZ = range(10)


class Place:
    def __init__(self):
        self.attn = lax.axis_index("attn")
        self.exp = lax.axis_index("exp")
        self.z = lax.div(self.attn, 2)
        self.y_lo = lax.rem(self.attn, 2)
        self.x = lax.div(self.exp, 4)
        self.y_hi = lax.rem(lax.div(self.exp, 2), 2)
        self.core = lax.rem(self.exp, 2)
        self.y = self.y_hi * 2 + self.y_lo
        self.group = lax.div(self.exp, 2)
        self.q = self.y_hi * 8 + self.y_lo * 4 + self.x
        self.partner = (self.attn, self.exp + 1 - 2 * self.core)

    def z_peer(self, d):
        other = lax.rem(self.z + d, 8)
        return other, (other * 2 + self.y_lo, self.exp)

    def plane_peer(self, d):
        other = lax.rem(self.q + d, 16)
        y_hi, y_lo, x = lax.div(other, 8), lax.rem(lax.div(other, 4), 2), lax.rem(other, 4)
        return other, (self.z * 2 + y_lo, (x * 2 + y_hi) * 2 + self.core)

    def exp_peer(self, d):
        other = lax.rem(self.exp + d, 16)
        return other, (self.attn, other)

    def group_peer(self, d):
        other = lax.rem(self.group + d, 8)
        return other, (self.attn, other * 2 + self.core)


def remote(src, dst, send_sem, recv_sem, device):
    return pltpu.make_async_remote_copy(
        src_ref=src,
        dst_ref=dst,
        send_sem=send_sem,
        recv_sem=recv_sem,
        device_id=device,
        device_id_type=MESH,
    )


def fill(ref, values):
    width = values.shape[-1]
    if width == ref.shape[-1]:
        ref[...] = values
    else:
        ref[..., 0:width] = values
        ref[..., width:] = jnp.zeros((*values.shape[:-1], ref.shape[-1] - width), values.dtype)


def wait_bytes(ref, sem):
    pltpu.make_async_copy(ref, ref, sem).wait()


def pipelined(count, stages, times):
    order = [
        (first + pitch * c, late, c, stage)
        for late, (stage, (first, pitch)) in enumerate(zip(stages, times))
        for c in range(count)
    ]
    for _, _, c, stage in sorted(order, key=lambda entry: entry[:3]):
        stage(c)


def layer(
    context,
    sinks,
    hidden_hbm,
    w_in_hbm,
    gain_in_hbm,
    keys_hbm,
    values_hbm,
    w_out_hbm,
    gain_hbm,
    index_hbm,
    share_hbm,
    gate_hbm,
    up_hbm,
    down_hbm,
    out,
    *scratch,
):
    s = SimpleNamespace(**dict(zip(SCRATCH, scratch)))
    rest = iter(scratch[len(SCRATCH) :])
    part = SimpleNamespace(
        **{name: [next(rest) for _ in range(n)] for name, (n, _, _) in CHUNKED.items()}
    )
    me = Place()
    core = me.core

    def send(way, c, src, dst, device):
        copy = remote(src, dst, s.send_sem.at[way, c], s.recv_sem.at[way, c], device)
        copy.start()
        return copy

    loads = SimpleNamespace()
    for number, (name, source) in enumerate(
        dict(
            hidden=hidden_hbm,
            w_in=w_in_hbm,
            gain_in=gain_in_hbm,
            keys=keys_hbm,
            values=values_hbm,
            w_out=w_out_hbm,
            gain=gain_hbm,
            index=index_hbm,
            share=share_hbm,
            gate=gate_hbm,
            up=up_hbm,
            down=down_hbm,
        ).items()
    ):
        load = pltpu.make_async_copy(source, getattr(s, name), s.load_sem.at[number])
        setattr(loads, name, load)
    loads.hidden.start()
    loads.w_in.start()
    loads.gain_in.start()
    loads.gain.start()
    loads.index.start()
    loads.share.start()

    barrier = pltpu.get_barrier_semaphore()

    def greet(device):
        pl.semaphore_signal(barrier, inc=1, device_id=device, device_id_type=MESH)

    @pl.loop(1, 8)
    def _(d):
        greet(me.z_peer(d)[1])

    @pl.loop(1, 16)
    def _(d):
        greet(me.plane_peer(d)[1])

    @pl.loop(0, 8)
    def _(g):
        greet((me.attn, g * 2 + 1 - core))

    loads.w_in.wait()
    loads.gain_in.wait()
    s.w_gain[...] = (s.w_in[...].astype(F32) * s.gain_in[...][None, :]).astype(BF)
    loads.hidden.wait()
    for load in (loads.keys, loads.values, loads.w_out, loads.gate, loads.up, loads.down):
        load.start()
    projected = jnp.dot(s.w_gain[...], s.hidden[...], preferred_element_type=F32)
    row_squares = jnp.zeros((8, 256), F32)
    for first in range(0, D, 96):
        piece = s.hidden[first : first + 96, :].astype(F32)
        row_squares = row_squares + jnp.sum((piece * piece).reshape(12, 8, 256), axis=0)
    row_scale = lax.rsqrt(jnp.sum(row_squares, axis=0, keepdims=True) / D + 1e-05)
    projected = (projected * row_scale).astype(BF)
    wide = (
        lax.broadcasted_iota(jnp.int32, (256, 256), 0),
        lax.broadcasted_iota(jnp.int32, (256, 256), 1),
    )
    identity = jnp.where(wide[0] == wide[1], 1.0, 0.0).astype(BF)
    by_row = lax.dot_general(identity, projected, NT, preferred_element_type=F32).astype(BF)
    fill(s.proj_out, by_row.reshape(16, 16, 160))
    lane = lax.broadcasted_iota(jnp.int32, (16, 128), 1)
    pair = lax.rem(lane, 32)
    row_of = lax.broadcasted_iota(jnp.int32, (16, 128), 0)
    position = jnp.zeros((16, 128), F32)
    for r in range(16):
        position = jnp.where(row_of == r, context[r].astype(F32), position)
    angle = position * jnp.exp(pair.astype(F32) * (-math.log(150000.0) / 32))
    sine = jnp.sin(angle)
    sine = jnp.where(lax.rem(lane, 64) < 32, -sine, sine)
    turn = jnp.where(lane < 64, jnp.cos(angle), sine)
    place_lane = lax.broadcasted_iota(jnp.int32, (1, 640), 1)
    entry = lax.rem(place_lane, 128)
    half = lax.rem(lax.div(entry, 32), 2)
    half = jnp.where(entry < 64, half, 1 - half)
    source = lax.div(place_lane, 128) * 64 + half * 32 + lax.rem(entry, 32)
    s.spreading[...] = jnp.where(
        lax.broadcasted_iota(jnp.int32, (320, 640), 0) == source, 1.0, 0.0
    ).astype(BF)
    head_row = lax.broadcasted_iota(jnp.int32, (32, 256), 0)
    head_lane = lax.broadcasted_iota(jnp.int32, (32, 256), 1)
    own_block = lax.div(head_lane, 64) == lax.div(head_row, 8)
    tail_row = lax.broadcasted_iota(jnp.int32, (8, 256), 0)
    tail_block = lax.div(lax.broadcasted_iota(jnp.int32, (8, 256), 1), 64)
    slot_number = lax.broadcasted_iota(jnp.int32, (32, 128), 1)
    parity = lax.div(slot_number, 64) == lax.rem(
        lax.broadcasted_iota(jnp.int32, (32, 128), 0), 2
    )
    sink_row = lax.broadcasted_iota(jnp.int32, (32, 1), 0)
    sink = jnp.zeros((32, 1), F32)
    for h in range(32):
        sink = jnp.where(sink_row == h, sinks[h], sink)

    loads.index.wait()
    loads.share.wait()
    loads.gain.wait()
    index, share = s.index, s.share
    slot = lax.broadcasted_iota(jnp.int32, (128, 16), 0)
    named = jnp.zeros((128, 16), F32)
    weight = jnp.zeros((128, 16), F32)
    for k in range(4):
        hit = index[k : k + 1, :] == lax.div(slot, 2)
        named = named + jnp.where(hit, 1.0, 0.0)
        weight = weight + jnp.where(hit, share[k : k + 1, :], 0.0)
    small_row = lax.broadcasted_iota(jnp.int32, (16, 16), 0)
    small_column = lax.broadcasted_iota(jnp.int32, (16, 16), 1)
    before = jnp.where(small_row < small_column, 1.0, 0.0).astype(BF)
    earlier = jnp.dot(named.astype(BF), before, preferred_element_type=F32)
    taken = jnp.where(earlier == lax.rem(slot, 2).astype(F32), named, 0.0)
    placing = taken.astype(BF)
    weight = weight * taken
    small_identity = jnp.where(small_row == small_column, 1.0, 0.0).astype(BF)

    def flipped(part_of):
        return lax.dot_general(small_identity, part_of, NT, preferred_element_type=F32).astype(BF)

    weight_hi = flipped(weight.astype(BF))
    weight_lo = flipped((weight - weight.astype(BF).astype(F32)).astype(BF))

    own_row = lax.broadcasted_iota(jnp.int32, (16, 256), 1) == (
        lax.broadcasted_iota(jnp.int32, (16, 256), 0) + me.exp * 16
    )
    own_row = jnp.where(own_row, 1.0, 0.0).astype(BF)
    for c0, width in CHUNKS:
        s.own_hidden[:, c0 : c0 + width] = lax.dot_general(
            own_row, s.hidden[c0 : c0 + width, :], NT, preferred_element_type=F32
        )

    by_source = lax.broadcasted_iota(jnp.int32, (1, 128), 1)
    by_source = (
        lax.div(lax.rem(by_source, 16), 2) * 16 + lax.div(by_source, 16) * 2 + lax.rem(by_source, 2)
    )
    wide_row = lax.broadcasted_iota(jnp.int32, (128, 128), 0)
    to_expert = jnp.where(by_source == wide_row, 1.0, 0.0).astype(BF)
    by_expert = lax.rem(lax.broadcasted_iota(jnp.int32, (1, 256), 1), 128)
    by_expert = (
        lax.div(lax.rem(by_expert, 16), 2) * 16 + lax.div(by_expert, 16) * 2 + lax.rem(by_expert, 2)
    )
    back_row = lax.broadcasted_iota(jnp.int32, (128, 256), 0)
    to_source = jnp.where(by_expert == back_row, 1.0, 0.0).astype(BF)

    pl.semaphore_wait(barrier, 30)

    @pl.loop(1, 16)
    def _(d):
        other, device = me.exp_peer(d)
        send(PA, 0, s.proj_out.at[other], s.proj_in.at[me.group, core], device)

    s.proj_in[me.group, core] = s.proj_out[me.exp]
    wait_bytes(s.proj_out.at[0:15], s.recv_sem.at[PA, 0])
    even = s.proj_in[:, 0].reshape(128, 256)[:, 0:160]
    odd = s.proj_in[:, 1].reshape(128, 256)[:, 0:160]
    laid = jnp.dot(even, s.spreading[0:160, :], preferred_element_type=F32) + jnp.dot(
        odd, s.spreading[160:320, :], preferred_element_type=F32
    )
    for t in range(5):
        plain = laid[:, t * 128 : (t + 1) * 128].reshape(8, 16, 128)
        turned = plain * turn[None]
        turned = turned + pltpu.roll(turned, 64, 2)
        for m in range(8):
            h = 5 * m + t
            block = turned[m]
            if h >= 36:
                block = jnp.where(lane < 64, plain[m], 0.0)
                block = block + pltpu.roll(block, 64, 1)
            s.heads[h * 16 : (h + 1) * 16, :] = block

    loads.keys.wait()
    loads.values.wait()
    for r in range(16):
        heads = s.heads[pl.ds(r, 40, stride=16), :]
        query = heads[0:32]
        query = jnp.where(own_block, jnp.concatenate([query, query], axis=1), 0.0)
        new = heads[32:40]
        new = jnp.concatenate([new, new], axis=1)
        new_key = jnp.sum(jnp.where(tail_block == tail_row, new, 0.0), axis=0, keepdims=True)
        new_value = jnp.sum(jnp.where(tail_block == tail_row - 4, new, 0.0), axis=0, keepdims=True)
        scores = (
            lax.dot_general(query.astype(BF), s.keys[r], NT, preferred_element_type=F32) * 0.125
        )
        own_score = jnp.sum(query * new_key, axis=1, keepdims=True) * 0.125
        valid = slot_number >= 128 - context[r]
        highest = jnp.maximum(
            jnp.max(jnp.where(valid, scores, -1e30), axis=1, keepdims=True),
            jnp.maximum(own_score, sink),
        )
        weights = jnp.where(valid, jnp.exp(scores - highest), 0.0)
        own_weight = jnp.exp(own_score - highest)
        denominator = (
            jnp.sum(weights, axis=1, keepdims=True) + own_weight + jnp.exp(sink - highest)
        )
        mixed = jnp.dot(weights.astype(BF), s.values[r], preferred_element_type=F32)
        mixed = (mixed + own_weight * new_value) / denominator
        mixed = jnp.where(own_block, mixed, 0.0)
        mixed = mixed[:, 0:128] + mixed[:, 128:256]
        mixed = mixed + pltpu.roll(mixed, 64, 1)
        s.mixed[pl.ds(r, 32, stride=16), :] = jnp.where(parity, mixed, 0.0)
    s.att_out[...] = jnp.sum(s.mixed[...].reshape(16, 2, 16, 128), axis=1).astype(BF)

    @pl.loop(1, 16)
    def _(d):
        other, device = me.exp_peer(d)
        send(AA, 0, s.att_out.at[other], s.att.at[me.group, core], device)

    s.att[me.group, core] = s.att_out[me.exp]

    wait_bytes(s.att_out.at[0:15], s.recv_sem.at[AA, 0])
    att = s.att
    loads.w_out.wait()

    core_copies = []
    att_mine = att[:, pl.ds(core, 1)].reshape(128, 128)
    att_other = att[:, pl.ds(1 - core, 1)].reshape(128, 128)
    for c, (c0, width) in enumerate(CHUNKS):
        shares = lax.dot_general(
            att_other, s.w_out[c0 : c0 + width, :], NT, preferred_element_type=F32
        )
        fill(part.rcs[c], shares.astype(BF))
        core_copies.append(send(RC, c, part.rcs[c], part.rcr[c], me.partner))
    for c, (c0, width) in enumerate(CHUNKS):
        shares = lax.dot_general(
            att_mine, s.w_out[c0 : c0 + width, :], NT, preferred_element_type=F32
        )
        fill(part.rmine[c], shares)

    squares = []
    swap_copies = {}

    def group_out(c):
        if c == NC:
            return
        width = WIDTHS[c]
        core_copies[c].wait_recv()
        total = part.rmine[c][...] + part.rcr[c][...].astype(F32)
        part.rsum[c][...] = total.astype(BF).reshape(8, 16, width)

        @pl.loop(1, 8)
        def _(d):
            other, device = me.group_peer(d)
            send(RS, c, part.rsum[c].at[other], part.rrec[c].at[me.group], device)

        part.rrec[c][me.group] = part.rsum[c][me.group]

    def z_out(c):
        width = WIDTHS[c]
        if c < NC:
            c0, width = CHUNKS[c]
            wait_bytes(part.rrec[c].at[0:7], s.recv_sem.at[RS, c])
            residual = s.own_hidden[:, c0 : c0 + width] + jnp.sum(
                part.rrec[c][:, :, 0:width].astype(F32), axis=0
            )
            s.residual[:, c0 : c0 + width] = residual
            squares.append(jnp.sum(residual * residual, axis=1, keepdims=True))
            outgoing = (residual * s.gain[c0 : c0 + width][None, :]).astype(BF)
        else:
            scale = lax.rsqrt(sum(squares) / D + 1e-05) + jnp.zeros((16, 128), F32)
            scale_hi = scale.astype(BF)
            scale_lo = (scale - scale_hi.astype(F32)).astype(BF)
            outgoing = jnp.where(lane < 64, scale_hi.astype(F32), scale_lo.astype(F32)).astype(
                BF
            )
        placed = jnp.dot(placing, outgoing, preferred_element_type=F32).astype(BF)
        fill(part.zs[c], placed.reshape(8, 16, width))

        @pl.loop(1, 8)
        def _(d):
            other, device = me.z_peer(d)
            send(Z, c, part.zs[c].at[other], part.zr[c].at[me.z], device)

        part.zr[c][me.z] = part.zs[c][me.z]

    def plane_out(c):
        width = WIDTHS[c]
        wait_bytes(part.zr[c].at[0:7], s.recv_sem.at[Z, c])
        rows = part.zr[c][...].reshape(128, width)
        placed = jnp.dot(to_expert, rows, preferred_element_type=F32).astype(BF)
        part.ps[c][...] = placed.reshape(8, 16, width)

        @pl.loop(1, 16)
        def _(d):
            other, device = me.plane_peer(d)
            send(
                PLANE, c, part.ps[c].at[lax.rem(other, 8)], part.xin[c].at[core, me.q], device
            )

        part.xin[c][core, me.q] = part.ps[c][lax.rem(me.q, 8)]

    def swap_out(c):
        wait_bytes(part.xin[c].at[0, 0:15], s.recv_sem.at[PLANE, c])
        mine = part.xin[c].at[core]
        swap_copies[c] = send(SWAP, c, mine, mine, me.partner)

    def hidden_units(c):
        swap_copies[c].wait_recv()
        if c == NC:
            return
        c0, width = CHUNKS[c]
        if c == 0:
            loads.gate.wait()
            loads.up.wait()
        rows = part.xin[c][...].reshape(512, WIDTHS[c])[:, 0:width]
        for weights, total in ((s.gate, s.gate_out), (s.up, s.up_out)):
            product = lax.dot_general(
                rows, weights[:, c0 : c0 + width], NT, preferred_element_type=F32
            )
            if c == 0:
                total[...] = product
            else:
                total[...] += product

    pipelined(NC + 1, (group_out, z_out, plane_out, swap_out, hidden_units), DISPATCH_TIMES)

    scales = part.xin[NC][...].reshape(512, 128).astype(F32)
    scales = scales[:, 0:1] + scales[:, 64:65]
    gate_out = s.gate_out[...] * scales
    up_out = s.up_out[...] * scales
    s.active[...] = (gate_out / (1.0 + jnp.exp(-gate_out)) * up_out).astype(BF)
    loads.down.wait()

    back_copies = {}

    def expert_out(c):
        c0, width = CHUNKS[c]
        columns = s.down[:, c0 : c0 + width]
        other_rows = s.active[pl.ds(pl.multiple_of((1 - core) * 256, 256), 256), :]
        results = jnp.dot(other_rows, columns, preferred_element_type=F32)
        fill(part.ycs[c], results.astype(BF))
        back_copies[c] = send(BC, c, part.ycs[c], part.ycr[c], me.partner)
        my_rows = s.active[pl.ds(pl.multiple_of(core * 256, 256), 256), :]
        fill(part.ymine[c], jnp.dot(my_rows, columns, preferred_element_type=F32))

    def plane_back(c):
        width = WIDTHS[c]
        back_copies[c].wait_recv()
        total = part.ymine[c][...] + part.ycr[c][...].astype(F32)
        part.ysum[c][...] = total.astype(BF).reshape(16, 16, width)

        @pl.loop(1, 16)
        def _(d):
            other, device = me.plane_peer(d)
            send(BP, c, part.ysum[c].at[other], part.pr[c].at[me.q], device)

        part.pr[c][me.q] = part.ysum[c][me.q]

    def z_back(c):
        width = WIDTHS[c]
        wait_bytes(part.pr[c].at[0:15], s.recv_sem.at[BP, c])
        rows = part.pr[c][...].reshape(256, width)
        part.vs[c][...] = (
            jnp.dot(to_source, rows, preferred_element_type=F32).astype(BF).reshape(8, 16, width)
        )

        @pl.loop(1, 8)
        def _(d):
            other, device = me.z_peer(d)
            send(BZ, c, part.vs[c].at[other], part.vr[c].at[me.z], device)

        part.vr[c][me.z] = part.vs[c][me.z]

    def finish(c):
        c0, width = CHUNKS[c]
        wait_bytes(part.vr[c].at[0:7], s.recv_sem.at[BZ, c])
        rows = part.vr[c][...].reshape(128, WIDTHS[c])[:, 0:width]
        mixed = jnp.dot(weight_hi, rows, preferred_element_type=F32) + jnp.dot(
            weight_lo, rows, preferred_element_type=F32
        )
        out[:, c0 : c0 + width] = (s.residual[:, c0 : c0 + width] + mixed).astype(BF)

    pipelined(NC, (expert_out, plane_back, z_back, finish), RETURN_TIMES)

    wait_bytes(s.proj_out.at[0:15], s.send_sem.at[PA, 0])
    wait_bytes(s.att_out.at[0:15], s.send_sem.at[AA, 0])
    for c in range(NC + 1):
        wait_bytes(part.zs[c].at[0:7], s.send_sem.at[Z, c])
        wait_bytes(part.xin[c].at[0, 0:15], s.send_sem.at[PLANE, c])
        swap_copies[c].wait_send()
    for c in range(NC):
        core_copies[c].wait_send()
        back_copies[c].wait_send()
        wait_bytes(part.rsum[c].at[0:7], s.send_sem.at[RS, c])
        wait_bytes(part.ysum[c].at[0:15], s.send_sem.at[BP, c])
        wait_bytes(part.vs[c].at[0:7], s.send_sem.at[BZ, c])


CHUNKED = dict(
    rcs=(NC, (128,), BF),
    rcr=(NC, (128,), BF),
    rmine=(NC, (128,), F32),
    rsum=(NC, (8, 16), BF),
    rrec=(NC, (8, 16), BF),
    zs=(NC + 1, (8, 16), BF),
    zr=(NC + 1, (8, 16), BF),
    ps=(NC + 1, (8, 16), BF),
    xin=(NC + 1, (2, 16, 16), BF),
    ycs=(NC, (256,), BF),
    ycr=(NC, (256,), BF),
    ymine=(NC, (256,), F32),
    ysum=(NC, (16, 16), BF),
    pr=(NC, (16, 16), BF),
    vs=(NC, (8, 16), BF),
    vr=(NC, (8, 16), BF),
)
SCRATCH = dict(
    hidden=pltpu.VMEM((D, 256), BF),
    w_in=pltpu.VMEM((160, D), BF),
    w_gain=pltpu.VMEM((160, D), BF),
    gain_in=pltpu.VMEM((D,), F32),
    keys=pltpu.VMEM((16, 128, 256), BF),
    values=pltpu.VMEM((16, 128, 256), BF),
    proj_out=pltpu.VMEM((16, 16, 256), BF),
    proj_in=pltpu.VMEM((8, 2, 16, 256), BF),
    spreading=pltpu.VMEM((320, 640), BF),
    heads=pltpu.VMEM((640, 128), F32),
    mixed=pltpu.VMEM((512, 128), F32),
    att_out=pltpu.VMEM((16, 16, 128), BF),
    att=pltpu.VMEM((8, 2, 16, 128), BF),
    own_hidden=pltpu.VMEM((16, D), F32),
    w_out=pltpu.VMEM((D, 128), BF),
    gain=pltpu.VMEM((D,), F32),
    index=pltpu.VMEM((4, 16), jnp.int32),
    share=pltpu.VMEM((4, 16), F32),
    gate=pltpu.VMEM((FFQ, D), BF),
    up=pltpu.VMEM((FFQ, D), BF),
    down=pltpu.VMEM((FFQ, D), BF),
    residual=pltpu.VMEM((16, D), F32),
    gate_out=pltpu.VMEM((512, FFQ), F32),
    up_out=pltpu.VMEM((512, FFQ), F32),
    active=pltpu.VMEM((512, FFQ), BF),
    load_sem=pltpu.SemaphoreType.DMA((12,)),
    send_sem=pltpu.SemaphoreType.DMA((10, NC + 1)),
    recv_sem=pltpu.SemaphoreType.DMA((10, NC + 1)),
)
PARTS = [
    pltpu.VMEM((*lead, WIDTHS[c]), dtype) for n, lead, dtype in CHUNKED.values() for c in range(n)
]


def per_device(
    hidden_rows,
    attention_gain,
    input_weight,
    cache_keys,
    cache_values,
    context_length,
    sink_logits,
    out_weight,
    expert_gain,
    expert_index,
    expert_share,
    gate_weight,
    up_weight,
    down_weight,
):
    scalars = pl.BlockSpec(memory_space=pltpu.SMEM)
    anywhere = pl.BlockSpec(memory_space=pltpu.HBM)
    return pl.pallas_call(
        layer,
        out_shape=jax.ShapeDtypeStruct((16, D), BF),
        in_specs=[scalars] * 2 + [anywhere] * 12,
        out_specs=pl.BlockSpec(memory_space=pltpu.VMEM),
        scratch_shapes=list(SCRATCH.values()) + PARTS,
        compiler_params=pltpu.CompilerParams(
            collective_id=0, has_side_effects=True, vmem_limit_bytes=60 * 1024 * 1024
        ),
        cost_estimate=pl.CostEstimate(
            flops=4_000_000_000, bytes_accessed=12_000_000, transcendentals=300_000
        ),
        name="layer",
    )(
        context_length,
        sink_logits,
        hidden_rows.T,
        input_weight.T,
        attention_gain,
        cache_keys,
        cache_values,
        out_weight.T,
        expert_gain,
        expert_index.T,
        expert_share.T,
        gate_weight,
        up_weight,
        down_weight,
    )


def solution(mesh):
    return jax.shard_map(
        per_device,
        mesh=mesh,
        in_specs=(
            P("attn", None),
            P(),
            P(None, "exp"),
            P(("attn", "exp"), None, None),
            P(("attn", "exp"), None, None),
            P(("attn", "exp")),
            P(),
            P("exp", None),
            P(),
            P(("attn", "exp"), None),
            P(("attn", "exp"), None),
            P(("attn", "exp"), None),
            P(("attn", "exp"), None),
            P(("attn", "exp"), None),
        ),
        out_specs=P(("attn", "exp"), None),
        check_vma=False,
    )
```

```python
import math
from types import SimpleNamespace

import jax
import jax.numpy as jnp
from jax import lax
from jax.experimental import pallas as pl
from jax.experimental.pallas import tpu as pltpu
from jax.sharding import PartitionSpec as P

D = 2880
FFQ = 360
CHUNKS = ((0, 512), (512, 512), (1024, 512), (1536, 512), (2048, 512), (2560, 320))
NC = len(CHUNKS)
DISPATCH_TIMES = ((0, 1), (2.1, 1), (5.2, 1), (8.3, 1), (9.4, 1))
RETURN_TIMES = ((0, 1), (1.1, 1), (4.2, 1), (7.3, 1))
WIDTHS = tuple((width + 127) // 128 * 128 for _, width in CHUNKS) + (128,)
BF = jnp.bfloat16
F32 = jnp.float32
MESH = pl.DeviceIdType.MESH
NT = (((1,), (1,)), ((), ()))
PA, AA, RC, RS, Z, PLANE, SWAP, BC, BP, BZ = range(10)


class Place:
    def __init__(self):
        self.attn = lax.axis_index("attn")
        self.exp = lax.axis_index("exp")
        self.z = lax.div(self.attn, 2)
        self.y_lo = lax.rem(self.attn, 2)
        self.x = lax.div(self.exp, 4)
        self.y_hi = lax.rem(lax.div(self.exp, 2), 2)
        self.core = lax.rem(self.exp, 2)
        self.y = self.y_hi * 2 + self.y_lo
        self.group = lax.div(self.exp, 2)
        self.q = self.y_hi * 8 + self.y_lo * 4 + self.x
        self.partner = (self.attn, self.exp + 1 - 2 * self.core)

    def z_peer(self, d):
        other = lax.rem(self.z + d, 8)
        return other, (other * 2 + self.y_lo, self.exp)

    def plane_peer(self, d):
        other = lax.rem(self.q + d, 16)
        y_hi, y_lo, x = lax.div(other, 8), lax.rem(lax.div(other, 4), 2), lax.rem(other, 4)
        return other, (self.z * 2 + y_lo, (x * 2 + y_hi) * 2 + self.core)

    def exp_peer(self, d):
        other = lax.rem(self.exp + d, 16)
        return other, (self.attn, other)

    def group_peer(self, d):
        other = lax.rem(self.group + d, 8)
        return other, (self.attn, other * 2 + self.core)


def remote(src, dst, send_sem, recv_sem, device):
    return pltpu.make_async_remote_copy(
        src_ref=src,
        dst_ref=dst,
        send_sem=send_sem,
        recv_sem=recv_sem,
        device_id=device,
        device_id_type=MESH,
    )


def fill(ref, values):
    width = values.shape[-1]
    if width == ref.shape[-1]:
        ref[...] = values
    else:
        ref[..., 0:width] = values
        ref[..., width:] = jnp.zeros((*values.shape[:-1], ref.shape[-1] - width), values.dtype)


def wait_bytes(ref, sem):
    pltpu.make_async_copy(ref, ref, sem).wait()


def pipelined(count, stages, times):
    order = [
        (first + pitch * c, late, c, stage)
        for late, (stage, (first, pitch)) in enumerate(zip(stages, times))
        for c in range(count)
    ]
    for _, _, c, stage in sorted(order, key=lambda entry: entry[:3]):
        stage(c)


def layer(
    context,
    sinks,
    hidden_hbm,
    w_in_hbm,
    gain_in_hbm,
    keys_hbm,
    values_hbm,
    w_out_hbm,
    gain_hbm,
    index_hbm,
    share_hbm,
    gate_hbm,
    up_hbm,
    down_hbm,
    out,
    *scratch,
):
    s = SimpleNamespace(**dict(zip(SCRATCH, scratch)))
    rest = iter(scratch[len(SCRATCH) :])
    part = SimpleNamespace(
        **{name: [next(rest) for _ in range(n)] for name, (n, _, _) in CHUNKED.items()}
    )
    me = Place()
    core = me.core

    def send(way, c, src, dst, device):
        copy = remote(src, dst, s.send_sem.at[way, c], s.recv_sem.at[way, c], device)
        copy.start()
        return copy

    loads = SimpleNamespace()
    for number, (name, source) in enumerate(
        dict(
            hidden=hidden_hbm,
            w_in=w_in_hbm,
            gain_in=gain_in_hbm,
            keys=keys_hbm,
            values=values_hbm,
            w_out=w_out_hbm,
            gain=gain_hbm,
            index=index_hbm,
            share=share_hbm,
            gate=gate_hbm,
            up=up_hbm,
            down=down_hbm,
        ).items()
    ):
        load = pltpu.make_async_copy(source, getattr(s, name), s.load_sem.at[number])
        setattr(loads, name, load)
    loads.hidden.start()
    loads.w_in.start()
    loads.gain_in.start()
    loads.gain.start()
    loads.index.start()
    loads.share.start()

    barrier = pltpu.get_barrier_semaphore()

    def greet(device):
        pl.semaphore_signal(barrier, inc=1, device_id=device, device_id_type=MESH)

    @pl.loop(1, 8)
    def _(d):
        greet(me.z_peer(d)[1])

    @pl.loop(1, 16)
    def _(d):
        greet(me.plane_peer(d)[1])

    @pl.loop(0, 8)
    def _(g):
        greet((me.attn, g * 2 + 1 - core))

    loads.w_in.wait()
    loads.gain_in.wait()
    s.w_gain[...] = (s.w_in[...].astype(F32) * s.gain_in[...][None, :]).astype(BF)
    loads.hidden.wait()
    for load in (loads.keys, loads.values, loads.w_out, loads.gate, loads.up, loads.down):
        load.start()
    projected = jnp.dot(s.w_gain[...], s.hidden[...], preferred_element_type=F32)
    row_squares = jnp.zeros((8, 256), F32)
    for first in range(0, D, 96):
        piece = s.hidden[first : first + 96, :].astype(F32)
        row_squares = row_squares + jnp.sum((piece * piece).reshape(12, 8, 256), axis=0)
    row_scale = lax.rsqrt(jnp.sum(row_squares, axis=0, keepdims=True) / D + 1e-05)
    projected = (projected * row_scale).astype(BF)
    wide = (
        lax.broadcasted_iota(jnp.int32, (256, 256), 0),
        lax.broadcasted_iota(jnp.int32, (256, 256), 1),
    )
    identity = jnp.where(wide[0] == wide[1], 1.0, 0.0).astype(BF)
    by_row = lax.dot_general(identity, projected, NT, preferred_element_type=F32).astype(BF)
    fill(s.proj_out, by_row.reshape(16, 16, 160))
    lane = lax.broadcasted_iota(jnp.int32, (16, 128), 1)
    pair = lax.rem(lane, 32)
    row_of = lax.broadcasted_iota(jnp.int32, (16, 128), 0)
    position = jnp.zeros((16, 128), F32)
    for r in range(16):
        position = jnp.where(row_of == r, context[r].astype(F32), position)
    angle = position * jnp.exp(pair.astype(F32) * (-math.log(150000.0) / 32))
    sine = jnp.sin(angle)
    sine = jnp.where(lax.rem(lane, 64) < 32, -sine, sine)
    turn = jnp.where(lane < 64, jnp.cos(angle), sine)
    place_lane = lax.broadcasted_iota(jnp.int32, (1, 640), 1)
    entry = lax.rem(place_lane, 128)
    half = lax.rem(lax.div(entry, 32), 2)
    half = jnp.where(entry < 64, half, 1 - half)
    source = lax.div(place_lane, 128) * 64 + half * 32 + lax.rem(entry, 32)
    s.spreading[...] = jnp.where(
        lax.broadcasted_iota(jnp.int32, (320, 640), 0) == source, 1.0, 0.0
    ).astype(BF)
    head_row = lax.broadcasted_iota(jnp.int32, (32, 256), 0)
    head_lane = lax.broadcasted_iota(jnp.int32, (32, 256), 1)
    own_block = lax.div(head_lane, 64) == lax.div(head_row, 8)
    tail_row = lax.broadcasted_iota(jnp.int32, (8, 256), 0)
    tail_block = lax.div(lax.broadcasted_iota(jnp.int32, (8, 256), 1), 64)
    slot_number = lax.broadcasted_iota(jnp.int32, (32, 128), 1)
    parity = lax.div(slot_number, 64) == lax.rem(
        lax.broadcasted_iota(jnp.int32, (32, 128), 0), 2
    )
    sink_row = lax.broadcasted_iota(jnp.int32, (32, 1), 0)
    sink = jnp.zeros((32, 1), F32)
    for h in range(32):
        sink = jnp.where(sink_row == h, sinks[h], sink)

    loads.index.wait()
    loads.share.wait()
    loads.gain.wait()
    index, share = s.index, s.share
    slot = lax.broadcasted_iota(jnp.int32, (128, 16), 0)
    named = jnp.zeros((128, 16), F32)
    weight = jnp.zeros((128, 16), F32)
    for k in range(4):
        hit = index[k : k + 1, :] == lax.div(slot, 2)
        named = named + jnp.where(hit, 1.0, 0.0)
        weight = weight + jnp.where(hit, share[k : k + 1, :], 0.0)
    small_row = lax.broadcasted_iota(jnp.int32, (16, 16), 0)
    small_column = lax.broadcasted_iota(jnp.int32, (16, 16), 1)
    before = jnp.where(small_row < small_column, 1.0, 0.0).astype(BF)
    earlier = jnp.dot(named.astype(BF), before, preferred_element_type=F32)
    taken = jnp.where(earlier == lax.rem(slot, 2).astype(F32), named, 0.0)
    placing = taken.astype(BF)
    weight = weight * taken
    small_identity = jnp.where(small_row == small_column, 1.0, 0.0).astype(BF)

    def flipped(part_of):
        return lax.dot_general(small_identity, part_of, NT, preferred_element_type=F32).astype(BF)

    weight_hi = flipped(weight.astype(BF))
    weight_lo = flipped((weight - weight.astype(BF).astype(F32)).astype(BF))

    own_row = lax.broadcasted_iota(jnp.int32, (16, 256), 1) == (
        lax.broadcasted_iota(jnp.int32, (16, 256), 0) + me.exp * 16
    )
    own_row = jnp.where(own_row, 1.0, 0.0).astype(BF)
    for c0, width in CHUNKS:
        s.own_hidden[:, c0 : c0 + width] = lax.dot_general(
            own_row, s.hidden[c0 : c0 + width, :], NT, preferred_element_type=F32
        )

    by_source = lax.broadcasted_iota(jnp.int32, (1, 128), 1)
    by_source = (
        lax.div(lax.rem(by_source, 16), 2) * 16 + lax.div(by_source, 16) * 2 + lax.rem(by_source, 2)
    )
    wide_row = lax.broadcasted_iota(jnp.int32, (128, 128), 0)
    to_expert = jnp.where(by_source == wide_row, 1.0, 0.0).astype(BF)
    by_expert = lax.rem(lax.broadcasted_iota(jnp.int32, (1, 256), 1), 128)
    by_expert = (
        lax.div(lax.rem(by_expert, 16), 2) * 16 + lax.div(by_expert, 16) * 2 + lax.rem(by_expert, 2)
    )
    back_row = lax.broadcasted_iota(jnp.int32, (128, 256), 0)
    to_source = jnp.where(by_expert == back_row, 1.0, 0.0).astype(BF)

    pl.semaphore_wait(barrier, 30)

    @pl.loop(1, 16)
    def _(d):
        other, device = me.exp_peer(d)
        send(PA, 0, s.proj_out.at[other], s.proj_in.at[me.group, core], device)

    s.proj_in[me.group, core] = s.proj_out[me.exp]
    wait_bytes(s.proj_out.at[0:15], s.recv_sem.at[PA, 0])
    even = s.proj_in[:, 0].reshape(128, 256)[:, 0:160]
    odd = s.proj_in[:, 1].reshape(128, 256)[:, 0:160]
    laid = jnp.dot(even, s.spreading[0:160, :], preferred_element_type=F32) + jnp.dot(
        odd, s.spreading[160:320, :], preferred_element_type=F32
    )
    for t in range(5):
        plain = laid[:, t * 128 : (t + 1) * 128].reshape(8, 16, 128)
        turned = plain * turn[None]
        turned = turned + pltpu.roll(turned, 64, 2)
        for m in range(8):
            h = 5 * m + t
            block = turned[m]
            if h >= 36:
                block = jnp.where(lane < 64, plain[m], 0.0)
                block = block + pltpu.roll(block, 64, 1)
            s.heads[h * 16 : (h + 1) * 16, :] = block

    loads.keys.wait()
    loads.values.wait()
    for r in range(16):
        heads = s.heads[pl.ds(r, 40, stride=16), :]
        query = heads[0:32]
        query = jnp.where(own_block, jnp.concatenate([query, query], axis=1), 0.0)
        new = heads[32:40]
        new = jnp.concatenate([new, new], axis=1)
        new_key = jnp.sum(jnp.where(tail_block == tail_row, new, 0.0), axis=0, keepdims=True)
        new_value = jnp.sum(jnp.where(tail_block == tail_row - 4, new, 0.0), axis=0, keepdims=True)
        scores = (
            lax.dot_general(query.astype(BF), s.keys[r], NT, preferred_element_type=F32) * 0.125
        )
        own_score = jnp.sum(query * new_key, axis=1, keepdims=True) * 0.125
        valid = slot_number >= 128 - context[r]
        highest = jnp.maximum(
            jnp.max(jnp.where(valid, scores, -1e30), axis=1, keepdims=True),
            jnp.maximum(own_score, sink),
        )
        weights = jnp.where(valid, jnp.exp(scores - highest), 0.0)
        own_weight = jnp.exp(own_score - highest)
        denominator = (
            jnp.sum(weights, axis=1, keepdims=True) + own_weight + jnp.exp(sink - highest)
        )
        mixed = jnp.dot(weights.astype(BF), s.values[r], preferred_element_type=F32)
        mixed = (mixed + own_weight * new_value) / denominator
        mixed = jnp.where(own_block, mixed, 0.0)
        mixed = mixed[:, 0:128] + mixed[:, 128:256]
        mixed = mixed + pltpu.roll(mixed, 64, 1)
        s.mixed[pl.ds(r, 32, stride=16), :] = jnp.where(parity, mixed, 0.0)
    s.att_out[...] = jnp.sum(s.mixed[...].reshape(16, 2, 16, 128), axis=1).astype(BF)

    @pl.loop(1, 16)
    def _(d):
        other, device = me.exp_peer(d)
        send(AA, 0, s.att_out.at[other], s.att.at[me.group, core], device)

    s.att[me.group, core] = s.att_out[me.exp]

    wait_bytes(s.att_out.at[0:15], s.recv_sem.at[AA, 0])
    att = s.att
    loads.w_out.wait()

    core_copies = []
    att_mine = att[:, pl.ds(core, 1)].reshape(128, 128)
    att_other = att[:, pl.ds(1 - core, 1)].reshape(128, 128)
    for c, (c0, width) in enumerate(CHUNKS):
        shares = lax.dot_general(
            att_other, s.w_out[c0 : c0 + width, :], NT, preferred_element_type=F32
        )
        fill(part.rcs[c], shares.astype(BF))
        core_copies.append(send(RC, c, part.rcs[c], part.rcr[c], me.partner))
    for c, (c0, width) in enumerate(CHUNKS):
        shares = lax.dot_general(
            att_mine, s.w_out[c0 : c0 + width, :], NT, preferred_element_type=F32
        )
        fill(part.rmine[c], shares)

    squares = []
    swap_copies = {}

    def group_out(c):
        if c == NC:
            return
        width = WIDTHS[c]
        core_copies[c].wait_recv()
        total = part.rmine[c][...] + part.rcr[c][...].astype(F32)
        part.rsum[c][...] = total.astype(BF).reshape(8, 16, width)

        @pl.loop(1, 8)
        def _(d):
            other, device = me.group_peer(d)
            send(RS, c, part.rsum[c].at[other], part.rrec[c].at[me.group], device)

        part.rrec[c][me.group] = part.rsum[c][me.group]

    def z_out(c):
        width = WIDTHS[c]
        if c < NC:
            c0, width = CHUNKS[c]
            wait_bytes(part.rrec[c].at[0:7], s.recv_sem.at[RS, c])
            residual = s.own_hidden[:, c0 : c0 + width] + jnp.sum(
                part.rrec[c][:, :, 0:width].astype(F32), axis=0
            )
            s.residual[:, c0 : c0 + width] = residual
            squares.append(jnp.sum(residual * residual, axis=1, keepdims=True))
            outgoing = (residual * s.gain[c0 : c0 + width][None, :]).astype(BF)
        else:
            scale = lax.rsqrt(sum(squares) / D + 1e-05) + jnp.zeros((16, 128), F32)
            scale_hi = scale.astype(BF)
            scale_lo = (scale - scale_hi.astype(F32)).astype(BF)
            outgoing = jnp.where(lane < 64, scale_hi.astype(F32), scale_lo.astype(F32)).astype(
                BF
            )
        placed = jnp.dot(placing, outgoing, preferred_element_type=F32).astype(BF)
        fill(part.zs[c], placed.reshape(8, 16, width))

        @pl.loop(1, 8)
        def _(d):
            other, device = me.z_peer(d)
            send(Z, c, part.zs[c].at[other], part.zr[c].at[me.z], device)

        part.zr[c][me.z] = part.zs[c][me.z]

    def plane_out(c):
        width = WIDTHS[c]
        wait_bytes(part.zr[c].at[0:7], s.recv_sem.at[Z, c])
        rows = part.zr[c][...].reshape(128, width)
        placed = jnp.dot(to_expert, rows, preferred_element_type=F32).astype(BF)
        part.ps[c][...] = placed.reshape(8, 16, width)

        @pl.loop(1, 16)
        def _(d):
            other, device = me.plane_peer(d)
            send(
                PLANE, c, part.ps[c].at[lax.rem(other, 8)], part.xin[c].at[core, me.q], device
            )

        part.xin[c][core, me.q] = part.ps[c][lax.rem(me.q, 8)]

    def swap_out(c):
        wait_bytes(part.xin[c].at[0, 0:15], s.recv_sem.at[PLANE, c])
        mine = part.xin[c].at[core]
        swap_copies[c] = send(SWAP, c, mine, mine, me.partner)

    def hidden_units(c):
        swap_copies[c].wait_recv()
        if c == NC:
            return
        c0, width = CHUNKS[c]
        if c == 0:
            loads.gate.wait()
            loads.up.wait()
        rows = part.xin[c][...].reshape(512, WIDTHS[c])[:, 0:width]
        for weights, total in ((s.gate, s.gate_out), (s.up, s.up_out)):
            product = lax.dot_general(
                rows, weights[:, c0 : c0 + width], NT, preferred_element_type=F32
            )
            if c == 0:
                total[...] = product
            else:
                total[...] += product

    pipelined(NC + 1, (group_out, z_out, plane_out, swap_out, hidden_units), DISPATCH_TIMES)

    scales = part.xin[NC][...].reshape(512, 128).astype(F32)
    scales = scales[:, 0:1] + scales[:, 64:65]
    gate_out = s.gate_out[...] * scales
    up_out = s.up_out[...] * scales
    s.active[...] = (gate_out / (1.0 + jnp.exp(-gate_out)) * up_out).astype(BF)
    loads.down.wait()

    back_copies = {}

    def expert_out(c):
        c0, width = CHUNKS[c]
        columns = s.down[:, c0 : c0 + width]
        other_rows = s.active[pl.ds(pl.multiple_of((1 - core) * 256, 256), 256), :]
        results = jnp.dot(other_rows, columns, preferred_element_type=F32)
        fill(part.ycs[c], results.astype(BF))
        back_copies[c] = send(BC, c, part.ycs[c], part.ycr[c], me.partner)
        my_rows = s.active[pl.ds(pl.multiple_of(core * 256, 256), 256), :]
        fill(part.ymine[c], jnp.dot(my_rows, columns, preferred_element_type=F32))

    def plane_back(c):
        width = WIDTHS[c]
        back_copies[c].wait_recv()
        total = part.ymine[c][...] + part.ycr[c][...].astype(F32)
        part.ysum[c][...] = total.astype(BF).reshape(16, 16, width)

        @pl.loop(1, 16)
        def _(d):
            other, device = me.plane_peer(d)
            send(BP, c, part.ysum[c].at[other], part.pr[c].at[me.q], device)

        part.pr[c][me.q] = part.ysum[c][me.q]

    def z_back(c):
        width = WIDTHS[c]
        wait_bytes(part.pr[c].at[0:15], s.recv_sem.at[BP, c])
        rows = part.pr[c][...].reshape(256, width)
        part.vs[c][...] = (
            jnp.dot(to_source, rows, preferred_element_type=F32).astype(BF).reshape(8, 16, width)
        )

        @pl.loop(1, 8)
        def _(d):
            other, device = me.z_peer(d)
            send(BZ, c, part.vs[c].at[other], part.vr[c].at[me.z], device)

        part.vr[c][me.z] = part.vs[c][me.z]

    def finish(c):
        c0, width = CHUNKS[c]
        wait_bytes(part.vr[c].at[0:7], s.recv_sem.at[BZ, c])
        rows = part.vr[c][...].reshape(128, WIDTHS[c])[:, 0:width]
        mixed = jnp.dot(weight_hi, rows, preferred_element_type=F32) + jnp.dot(
            weight_lo, rows, preferred_element_type=F32
        )
        out[:, c0 : c0 + width] = (s.residual[:, c0 : c0 + width] + mixed).astype(BF)

    pipelined(NC, (expert_out, plane_back, z_back, finish), RETURN_TIMES)

    wait_bytes(s.proj_out.at[0:15], s.send_sem.at[PA, 0])
    wait_bytes(s.att_out.at[0:15], s.send_sem.at[AA, 0])
    for c in range(NC + 1):
        wait_bytes(part.zs[c].at[0:7], s.send_sem.at[Z, c])
        wait_bytes(part.xin[c].at[0, 0:15], s.send_sem.at[PLANE, c])
        swap_copies[c].wait_send()
    for c in range(NC):
        core_copies[c].wait_send()
        back_copies[c].wait_send()
        wait_bytes(part.rsum[c].at[0:7], s.send_sem.at[RS, c])
        wait_bytes(part.ysum[c].at[0:15], s.send_sem.at[BP, c])
        wait_bytes(part.vs[c].at[0:7], s.send_sem.at[BZ, c])


CHUNKED = dict(
    rcs=(NC, (128,), BF),
    rcr=(NC, (128,), BF),
    rmine=(NC, (128,), F32),
    rsum=(NC, (8, 16), BF),
    rrec=(NC, (8, 16), BF),
    zs=(NC + 1, (8, 16), BF),
    zr=(NC + 1, (8, 16), BF),
    ps=(NC + 1, (8, 16), BF),
    xin=(NC + 1, (2, 16, 16), BF),
    ycs=(NC, (256,), BF),
    ycr=(NC, (256,), BF),
    ymine=(NC, (256,), F32),
    ysum=(NC, (16, 16), BF),
    pr=(NC, (16, 16), BF),
    vs=(NC, (8, 16), BF),
    vr=(NC, (8, 16), BF),
)
SCRATCH = dict(
    hidden=pltpu.VMEM((D, 256), BF),
    w_in=pltpu.VMEM((160, D), BF),
    w_gain=pltpu.VMEM((160, D), BF),
    gain_in=pltpu.VMEM((D,), F32),
    keys=pltpu.VMEM((16, 128, 256), BF),
    values=pltpu.VMEM((16, 128, 256), BF),
    proj_out=pltpu.VMEM((16, 16, 256), BF),
    proj_in=pltpu.VMEM((8, 2, 16, 256), BF),
    spreading=pltpu.VMEM((320, 640), BF),
    heads=pltpu.VMEM((640, 128), F32),
    mixed=pltpu.VMEM((512, 128), F32),
    att_out=pltpu.VMEM((16, 16, 128), BF),
    att=pltpu.VMEM((8, 2, 16, 128), BF),
    own_hidden=pltpu.VMEM((16, D), F32),
    w_out=pltpu.VMEM((D, 128), BF),
    gain=pltpu.VMEM((D,), F32),
    index=pltpu.VMEM((4, 16), jnp.int32),
    share=pltpu.VMEM((4, 16), F32),
    gate=pltpu.VMEM((FFQ, D), BF),
    up=pltpu.VMEM((FFQ, D), BF),
    down=pltpu.VMEM((FFQ, D), BF),
    residual=pltpu.VMEM((16, D), F32),
    gate_out=pltpu.VMEM((512, FFQ), F32),
    up_out=pltpu.VMEM((512, FFQ), F32),
    active=pltpu.VMEM((512, FFQ), BF),
    load_sem=pltpu.SemaphoreType.DMA((12,)),
    send_sem=pltpu.SemaphoreType.DMA((10, NC + 1)),
    recv_sem=pltpu.SemaphoreType.DMA((10, NC + 1)),
)
PARTS = [
    pltpu.VMEM((*lead, WIDTHS[c]), dtype) for n, lead, dtype in CHUNKED.values() for c in range(n)
]


def per_device(
    hidden_rows,
    attention_gain,
    input_weight,
    cache_keys,
    cache_values,
    context_length,
    sink_logits,
    out_weight,
    expert_gain,
    expert_index,
    expert_share,
    gate_weight,
    up_weight,
    down_weight,
):
    scalars = pl.BlockSpec(memory_space=pltpu.SMEM)
    anywhere = pl.BlockSpec(memory_space=pltpu.HBM)
    return pl.pallas_call(
        layer,
        out_shape=jax.ShapeDtypeStruct((16, D), BF),
        in_specs=[scalars] * 2 + [anywhere] * 12,
        out_specs=pl.BlockSpec(memory_space=pltpu.VMEM),
        scratch_shapes=list(SCRATCH.values()) + PARTS,
        compiler_params=pltpu.CompilerParams(
            collective_id=0, has_side_effects=True, vmem_limit_bytes=60 * 1024 * 1024
        ),
        cost_estimate=pl.CostEstimate(
            flops=4_000_000_000, bytes_accessed=12_000_000, transcendentals=300_000
        ),
        name="layer",
    )(
        context_length,
        sink_logits,
        hidden_rows.T,
        input_weight.T,
        attention_gain,
        cache_keys,
        cache_values,
        out_weight.T,
        expert_gain,
        expert_index.T,
        expert_share.T,
        gate_weight,
        up_weight,
        down_weight,
    )


def solution(mesh):
    return jax.shard_map(
        per_device,
        mesh=mesh,
        in_specs=(
            P("attn", None),
            P(),
            P(None, "exp"),
            P(("attn", "exp"), None, None),
            P(("attn", "exp"), None, None),
            P(("attn", "exp")),
            P(),
            P("exp", None),
            P(),
            P(("attn", "exp"), None),
            P(("attn", "exp"), None),
            P(("attn", "exp"), None),
            P(("attn", "exp"), None),
            P(("attn", "exp"), None),
        ),
        out_specs=P(("attn", "exp"), None),
        check_vma=False,
    )
```

```python
import math
from types import SimpleNamespace

import jax
import jax.numpy as jnp
from jax import lax
from jax.experimental import pallas as pl
from jax.experimental.pallas import tpu as pltpu
from jax.sharding import PartitionSpec as P

D = 2880
FFQ = 360
CHUNKS = ((0, 512), (512, 512), (1024, 512), (1536, 512), (2048, 512), (2560, 320))
NC = len(CHUNKS)
DISPATCH_TIMES = ((0, 1), (2.1, 1), (5.2, 1), (9.3, 1), (10.4, 1))
RETURN_TIMES = ((0, 1), (1.1, 1), (5.2, 1), (9.3, 1))
WIDTHS = tuple((width + 127) // 128 * 128 for _, width in CHUNKS) + (128,)
BF = jnp.bfloat16
F32 = jnp.float32
MESH = pl.DeviceIdType.MESH
NT = (((1,), (1,)), ((), ()))
PA, AA, RC, RS, Z, PLANE, SWAP, BC, BP, BZ = range(10)


class Place:
    def __init__(self):
        self.attn = lax.axis_index("attn")
        self.exp = lax.axis_index("exp")
        self.z = lax.div(self.attn, 2)
        self.y_lo = lax.rem(self.attn, 2)
        self.x = lax.div(self.exp, 4)
        self.y_hi = lax.rem(lax.div(self.exp, 2), 2)
        self.core = lax.rem(self.exp, 2)
        self.y = self.y_hi * 2 + self.y_lo
        self.group = lax.div(self.exp, 2)
        self.q = self.y_hi * 8 + self.y_lo * 4 + self.x
        self.partner = (self.attn, self.exp + 1 - 2 * self.core)

    def z_peer(self, d):
        other = lax.rem(self.z + d, 8)
        return other, (other * 2 + self.y_lo, self.exp)

    def plane_peer(self, d):
        other = lax.rem(self.q + d, 16)
        y_hi, y_lo, x = lax.div(other, 8), lax.rem(lax.div(other, 4), 2), lax.rem(other, 4)
        return other, (self.z * 2 + y_lo, (x * 2 + y_hi) * 2 + self.core)

    def exp_peer(self, d):
        other = lax.rem(self.exp + d, 16)
        return other, (self.attn, other)

    def group_peer(self, d):
        other = lax.rem(self.group + d, 8)
        return other, (self.attn, other * 2 + self.core)


def remote(src, dst, send_sem, recv_sem, device):
    return pltpu.make_async_remote_copy(
        src_ref=src,
        dst_ref=dst,
        send_sem=send_sem,
        recv_sem=recv_sem,
        device_id=device,
        device_id_type=MESH,
    )


def fill(ref, values):
    width = values.shape[-1]
    if width == ref.shape[-1]:
        ref[...] = values
    else:
        ref[..., 0:width] = values
        ref[..., width:] = jnp.zeros((*values.shape[:-1], ref.shape[-1] - width), values.dtype)


def wait_bytes(ref, sem):
    pltpu.make_async_copy(ref, ref, sem).wait()


def pipelined(count, stages, times):
    order = [
        (first + pitch * c, late, c, stage)
        for late, (stage, (first, pitch)) in enumerate(zip(stages, times))
        for c in range(count)
    ]
    for _, _, c, stage in sorted(order, key=lambda entry: entry[:3]):
        stage(c)


def layer(
    context,
    sinks,
    hidden_hbm,
    w_in_hbm,
    gain_in_hbm,
    keys_hbm,
    values_hbm,
    w_out_hbm,
    gain_hbm,
    index_hbm,
    share_hbm,
    gate_hbm,
    up_hbm,
    down_hbm,
    out,
    *scratch,
):
    s = SimpleNamespace(**dict(zip(SCRATCH, scratch)))
    rest = iter(scratch[len(SCRATCH) :])
    part = SimpleNamespace(
        **{name: [next(rest) for _ in range(n)] for name, (n, _, _) in CHUNKED.items()}
    )
    me = Place()
    core = me.core

    def send(way, c, src, dst, device):
        copy = remote(src, dst, s.send_sem.at[way, c], s.recv_sem.at[way, c], device)
        copy.start()
        return copy

    loads = SimpleNamespace()
    for number, (name, source) in enumerate(
        dict(
            hidden=hidden_hbm,
            w_in=w_in_hbm,
            gain_in=gain_in_hbm,
            keys=keys_hbm,
            values=values_hbm,
            w_out=w_out_hbm,
            gain=gain_hbm,
            index=index_hbm,
            share=share_hbm,
            gate=gate_hbm,
            up=up_hbm,
            down=down_hbm,
        ).items()
    ):
        load = pltpu.make_async_copy(source, getattr(s, name), s.load_sem.at[number])
        setattr(loads, name, load)
    loads.hidden.start()
    loads.w_in.start()
    loads.gain_in.start()
    loads.gain.start()
    loads.index.start()
    loads.share.start()

    barrier = pltpu.get_barrier_semaphore()

    def greet(device):
        pl.semaphore_signal(barrier, inc=1, device_id=device, device_id_type=MESH)

    @pl.loop(1, 8)
    def _(d):
        greet(me.z_peer(d)[1])

    @pl.loop(1, 16)
    def _(d):
        greet(me.plane_peer(d)[1])

    @pl.loop(0, 8)
    def _(g):
        greet((me.attn, g * 2 + 1 - core))

    loads.w_in.wait()
    loads.gain_in.wait()
    s.w_gain[...] = (s.w_in[...].astype(F32) * s.gain_in[...][None, :]).astype(BF)
    loads.hidden.wait()
    for load in (loads.keys, loads.values, loads.w_out, loads.gate, loads.up, loads.down):
        load.start()
    projected = jnp.dot(s.w_gain[...], s.hidden[...], preferred_element_type=F32)
    row_squares = jnp.zeros((8, 256), F32)
    for first in range(0, D, 96):
        piece = s.hidden[first : first + 96, :].astype(F32)
        row_squares = row_squares + jnp.sum((piece * piece).reshape(12, 8, 256), axis=0)
    row_scale = lax.rsqrt(jnp.sum(row_squares, axis=0, keepdims=True) / D + 1e-05)
    projected = (projected * row_scale).astype(BF)
    wide = (
        lax.broadcasted_iota(jnp.int32, (256, 256), 0),
        lax.broadcasted_iota(jnp.int32, (256, 256), 1),
    )
    identity = jnp.where(wide[0] == wide[1], 1.0, 0.0).astype(BF)
    by_row = lax.dot_general(identity, projected, NT, preferred_element_type=F32).astype(BF)
    fill(s.proj_out, by_row.reshape(16, 16, 160))
    lane = lax.broadcasted_iota(jnp.int32, (16, 128), 1)
    pair = lax.rem(lane, 32)
    row_of = lax.broadcasted_iota(jnp.int32, (16, 128), 0)
    position = jnp.zeros((16, 128), F32)
    for r in range(16):
        position = jnp.where(row_of == r, context[r].astype(F32), position)
    angle = position * jnp.exp(pair.astype(F32) * (-math.log(150000.0) / 32))
    sine = jnp.sin(angle)
    sine = jnp.where(lax.rem(lane, 64) < 32, -sine, sine)
    turn = jnp.where(lane < 64, jnp.cos(angle), sine)
    place_lane = lax.broadcasted_iota(jnp.int32, (1, 640), 1)
    entry = lax.rem(place_lane, 128)
    half = lax.rem(lax.div(entry, 32), 2)
    half = jnp.where(entry < 64, half, 1 - half)
    source = lax.div(place_lane, 128) * 64 + half * 32 + lax.rem(entry, 32)
    s.spreading[...] = jnp.where(
        lax.broadcasted_iota(jnp.int32, (320, 640), 0) == source, 1.0, 0.0
    ).astype(BF)
    head_row = lax.broadcasted_iota(jnp.int32, (32, 256), 0)
    head_lane = lax.broadcasted_iota(jnp.int32, (32, 256), 1)
    own_block = lax.div(head_lane, 64) == lax.div(head_row, 8)
    tail_row = lax.broadcasted_iota(jnp.int32, (8, 256), 0)
    tail_block = lax.div(lax.broadcasted_iota(jnp.int32, (8, 256), 1), 64)
    slot_number = lax.broadcasted_iota(jnp.int32, (32, 128), 1)
    parity = lax.div(slot_number, 64) == lax.rem(
        lax.broadcasted_iota(jnp.int32, (32, 128), 0), 2
    )
    sink_row = lax.broadcasted_iota(jnp.int32, (32, 1), 0)
    sink = jnp.zeros((32, 1), F32)
    for h in range(32):
        sink = jnp.where(sink_row == h, sinks[h], sink)

    loads.index.wait()
    loads.share.wait()
    loads.gain.wait()
    index, share = s.index, s.share
    slot = lax.broadcasted_iota(jnp.int32, (128, 16), 0)
    named = jnp.zeros((128, 16), F32)
    weight = jnp.zeros((128, 16), F32)
    for k in range(4):
        hit = index[k : k + 1, :] == lax.div(slot, 2)
        named = named + jnp.where(hit, 1.0, 0.0)
        weight = weight + jnp.where(hit, share[k : k + 1, :], 0.0)
    small_row = lax.broadcasted_iota(jnp.int32, (16, 16), 0)
    small_column = lax.broadcasted_iota(jnp.int32, (16, 16), 1)
    before = jnp.where(small_row < small_column, 1.0, 0.0).astype(BF)
    earlier = jnp.dot(named.astype(BF), before, preferred_element_type=F32)
    taken = jnp.where(earlier == lax.rem(slot, 2).astype(F32), named, 0.0)
    placing = taken.astype(BF)
    weight = weight * taken
    small_identity = jnp.where(small_row == small_column, 1.0, 0.0).astype(BF)

    def flipped(part_of):
        return lax.dot_general(small_identity, part_of, NT, preferred_element_type=F32).astype(BF)

    weight_hi = flipped(weight.astype(BF))
    weight_lo = flipped((weight - weight.astype(BF).astype(F32)).astype(BF))

    own_row = lax.broadcasted_iota(jnp.int32, (16, 256), 1) == (
        lax.broadcasted_iota(jnp.int32, (16, 256), 0) + me.exp * 16
    )
    own_row = jnp.where(own_row, 1.0, 0.0).astype(BF)
    for c0, width in CHUNKS:
        s.own_hidden[:, c0 : c0 + width] = lax.dot_general(
            own_row, s.hidden[c0 : c0 + width, :], NT, preferred_element_type=F32
        )

    by_source = lax.broadcasted_iota(jnp.int32, (1, 128), 1)
    by_source = (
        lax.div(lax.rem(by_source, 16), 2) * 16 + lax.div(by_source, 16) * 2 + lax.rem(by_source, 2)
    )
    wide_row = lax.broadcasted_iota(jnp.int32, (128, 128), 0)
    to_expert = jnp.where(by_source == wide_row, 1.0, 0.0).astype(BF)
    by_expert = lax.rem(lax.broadcasted_iota(jnp.int32, (1, 256), 1), 128)
    by_expert = (
        lax.div(lax.rem(by_expert, 16), 2) * 16 + lax.div(by_expert, 16) * 2 + lax.rem(by_expert, 2)
    )
    back_row = lax.broadcasted_iota(jnp.int32, (128, 256), 0)
    to_source = jnp.where(by_expert == back_row, 1.0, 0.0).astype(BF)

    pl.semaphore_wait(barrier, 30)

    @pl.loop(1, 16)
    def _(d):
        other, device = me.exp_peer(d)
        send(PA, 0, s.proj_out.at[other], s.proj_in.at[me.group, core], device)

    s.proj_in[me.group, core] = s.proj_out[me.exp]
    wait_bytes(s.proj_out.at[0:15], s.recv_sem.at[PA, 0])
    even = s.proj_in[:, 0].reshape(128, 256)[:, 0:160]
    odd = s.proj_in[:, 1].reshape(128, 256)[:, 0:160]
    laid = jnp.dot(even, s.spreading[0:160, :], preferred_element_type=F32) + jnp.dot(
        odd, s.spreading[160:320, :], preferred_element_type=F32
    )
    for t in range(5):
        plain = laid[:, t * 128 : (t + 1) * 128].reshape(8, 16, 128)
        turned = plain * turn[None]
        turned = turned + pltpu.roll(turned, 64, 2)
        for m in range(8):
            h = 5 * m + t
            block = turned[m]
            if h >= 36:
                block = jnp.where(lane < 64, plain[m], 0.0)
                block = block + pltpu.roll(block, 64, 1)
            s.heads[h * 16 : (h + 1) * 16, :] = block

    loads.keys.wait()
    loads.values.wait()
    for r in range(16):
        heads = s.heads[pl.ds(r, 40, stride=16), :]
        query = heads[0:32]
        query = jnp.where(own_block, jnp.concatenate([query, query], axis=1), 0.0)
        new = heads[32:40]
        new = jnp.concatenate([new, new], axis=1)
        new_key = jnp.sum(jnp.where(tail_block == tail_row, new, 0.0), axis=0, keepdims=True)
        new_value = jnp.sum(jnp.where(tail_block == tail_row - 4, new, 0.0), axis=0, keepdims=True)
        scores = (
            lax.dot_general(query.astype(BF), s.keys[r], NT, preferred_element_type=F32) * 0.125
        )
        own_score = jnp.sum(query * new_key, axis=1, keepdims=True) * 0.125
        valid = slot_number >= 128 - context[r]
        highest = jnp.maximum(
            jnp.max(jnp.where(valid, scores, -1e30), axis=1, keepdims=True),
            jnp.maximum(own_score, sink),
        )
        weights = jnp.where(valid, jnp.exp(scores - highest), 0.0)
        own_weight = jnp.exp(own_score - highest)
        denominator = (
            jnp.sum(weights, axis=1, keepdims=True) + own_weight + jnp.exp(sink - highest)
        )
        mixed = jnp.dot(weights.astype(BF), s.values[r], preferred_element_type=F32)
        mixed = (mixed + own_weight * new_value) / denominator
        mixed = jnp.where(own_block, mixed, 0.0)
        mixed = mixed[:, 0:128] + mixed[:, 128:256]
        mixed = mixed + pltpu.roll(mixed, 64, 1)
        s.mixed[pl.ds(r, 32, stride=16), :] = jnp.where(parity, mixed, 0.0)
    s.att_out[...] = jnp.sum(s.mixed[...].reshape(16, 2, 16, 128), axis=1).astype(BF)

    @pl.loop(1, 16)
    def _(d):
        other, device = me.exp_peer(d)
        send(AA, 0, s.att_out.at[other], s.att.at[me.group, core], device)

    s.att[me.group, core] = s.att_out[me.exp]

    wait_bytes(s.att_out.at[0:15], s.recv_sem.at[AA, 0])
    att = s.att
    loads.w_out.wait()

    core_copies = []
    att_mine = att[:, pl.ds(core, 1)].reshape(128, 128)
    att_other = att[:, pl.ds(1 - core, 1)].reshape(128, 128)
    for c, (c0, width) in enumerate(CHUNKS):
        shares = lax.dot_general(
            att_other, s.w_out[c0 : c0 + width, :], NT, preferred_element_type=F32
        )
        fill(part.rcs[c], shares.astype(BF))
        core_copies.append(send(RC, c, part.rcs[c], part.rcr[c], me.partner))
    for c, (c0, width) in enumerate(CHUNKS):
        shares = lax.dot_general(
            att_mine, s.w_out[c0 : c0 + width, :], NT, preferred_element_type=F32
        )
        fill(part.rmine[c], shares)

    squares = []
    swap_copies = {}

    def group_out(c):
        if c == NC:
            return
        width = WIDTHS[c]
        core_copies[c].wait_recv()
        total = part.rmine[c][...] + part.rcr[c][...].astype(F32)
        part.rsum[c][...] = total.astype(BF).reshape(8, 16, width)

        @pl.loop(1, 8)
        def _(d):
            other, device = me.group_peer(d)
            send(RS, c, part.rsum[c].at[other], part.rrec[c].at[me.group], device)

        part.rrec[c][me.group] = part.rsum[c][me.group]

    def z_out(c):
        width = WIDTHS[c]
        if c < NC:
            c0, width = CHUNKS[c]
            wait_bytes(part.rrec[c].at[0:7], s.recv_sem.at[RS, c])
            residual = s.own_hidden[:, c0 : c0 + width] + jnp.sum(
                part.rrec[c][:, :, 0:width].astype(F32), axis=0
            )
            s.residual[:, c0 : c0 + width] = residual
            squares.append(jnp.sum(residual * residual, axis=1, keepdims=True))
            outgoing = (residual * s.gain[c0 : c0 + width][None, :]).astype(BF)
        else:
            scale = lax.rsqrt(sum(squares) / D + 1e-05) + jnp.zeros((16, 128), F32)
            scale_hi = scale.astype(BF)
            scale_lo = (scale - scale_hi.astype(F32)).astype(BF)
            outgoing = jnp.where(lane < 64, scale_hi.astype(F32), scale_lo.astype(F32)).astype(
                BF
            )
        placed = jnp.dot(placing, outgoing, preferred_element_type=F32).astype(BF)
        fill(part.zs[c], placed.reshape(8, 16, width))

        @pl.loop(1, 8)
        def _(d):
            other, device = me.z_peer(d)
            send(Z, c, part.zs[c].at[other], part.zr[c].at[me.z], device)

        part.zr[c][me.z] = part.zs[c][me.z]

    def plane_out(c):
        width = WIDTHS[c]
        wait_bytes(part.zr[c].at[0:7], s.recv_sem.at[Z, c])
        rows = part.zr[c][...].reshape(128, width)
        placed = jnp.dot(to_expert, rows, preferred_element_type=F32).astype(BF)
        part.ps[c][...] = placed.reshape(8, 16, width)

        @pl.loop(1, 16)
        def _(d):
            other, device = me.plane_peer(d)
            send(
                PLANE, c, part.ps[c].at[lax.rem(other, 8)], part.xin[c].at[core, me.q], device
            )

        part.xin[c][core, me.q] = part.ps[c][lax.rem(me.q, 8)]

    def swap_out(c):
        wait_bytes(part.xin[c].at[0, 0:15], s.recv_sem.at[PLANE, c])
        mine = part.xin[c].at[core]
        swap_copies[c] = send(SWAP, c, mine, mine, me.partner)

    def hidden_units(c):
        swap_copies[c].wait_recv()
        if c == NC:
            return
        c0, width = CHUNKS[c]
        if c == 0:
            loads.gate.wait()
            loads.up.wait()
        rows = part.xin[c][...].reshape(512, WIDTHS[c])[:, 0:width]
        for weights, total in ((s.gate, s.gate_out), (s.up, s.up_out)):
            product = lax.dot_general(
                rows, weights[:, c0 : c0 + width], NT, preferred_element_type=F32
            )
            if c == 0:
                total[...] = product
            else:
                total[...] += product

    pipelined(NC + 1, (group_out, z_out, plane_out, swap_out, hidden_units), DISPATCH_TIMES)

    scales = part.xin[NC][...].reshape(512, 128).astype(F32)
    scales = scales[:, 0:1] + scales[:, 64:65]
    gate_out = s.gate_out[...] * scales
    up_out = s.up_out[...] * scales
    s.active[...] = (gate_out / (1.0 + jnp.exp(-gate_out)) * up_out).astype(BF)
    loads.down.wait()

    back_copies = {}

    def expert_out(c):
        c0, width = CHUNKS[c]
        columns = s.down[:, c0 : c0 + width]
        other_rows = s.active[pl.ds(pl.multiple_of((1 - core) * 256, 256), 256), :]
        results = jnp.dot(other_rows, columns, preferred_element_type=F32)
        fill(part.ycs[c], results.astype(BF))
        back_copies[c] = send(BC, c, part.ycs[c], part.ycr[c], me.partner)
        my_rows = s.active[pl.ds(pl.multiple_of(core * 256, 256), 256), :]
        fill(part.ymine[c], jnp.dot(my_rows, columns, preferred_element_type=F32))

    def plane_back(c):
        width = WIDTHS[c]
        back_copies[c].wait_recv()
        total = part.ymine[c][...] + part.ycr[c][...].astype(F32)
        part.ysum[c][...] = total.astype(BF).reshape(16, 16, width)

        @pl.loop(1, 16)
        def _(d):
            other, device = me.plane_peer(d)
            send(BP, c, part.ysum[c].at[other], part.pr[c].at[me.q], device)

        part.pr[c][me.q] = part.ysum[c][me.q]

    def z_back(c):
        width = WIDTHS[c]
        wait_bytes(part.pr[c].at[0:15], s.recv_sem.at[BP, c])
        rows = part.pr[c][...].reshape(256, width)
        part.vs[c][...] = (
            jnp.dot(to_source, rows, preferred_element_type=F32).astype(BF).reshape(8, 16, width)
        )

        @pl.loop(1, 8)
        def _(d):
            other, device = me.z_peer(d)
            send(BZ, c, part.vs[c].at[other], part.vr[c].at[me.z], device)

        part.vr[c][me.z] = part.vs[c][me.z]

    def finish(c):
        c0, width = CHUNKS[c]
        wait_bytes(part.vr[c].at[0:7], s.recv_sem.at[BZ, c])
        rows = part.vr[c][...].reshape(128, WIDTHS[c])[:, 0:width]
        mixed = jnp.dot(weight_hi, rows, preferred_element_type=F32) + jnp.dot(
            weight_lo, rows, preferred_element_type=F32
        )
        out[:, c0 : c0 + width] = (s.residual[:, c0 : c0 + width] + mixed).astype(BF)

    pipelined(NC, (expert_out, plane_back, z_back, finish), RETURN_TIMES)

    wait_bytes(s.proj_out.at[0:15], s.send_sem.at[PA, 0])
    wait_bytes(s.att_out.at[0:15], s.send_sem.at[AA, 0])
    for c in range(NC + 1):
        wait_bytes(part.zs[c].at[0:7], s.send_sem.at[Z, c])
        wait_bytes(part.xin[c].at[0, 0:15], s.send_sem.at[PLANE, c])
        swap_copies[c].wait_send()
    for c in range(NC):
        core_copies[c].wait_send()
        back_copies[c].wait_send()
        wait_bytes(part.rsum[c].at[0:7], s.send_sem.at[RS, c])
        wait_bytes(part.ysum[c].at[0:15], s.send_sem.at[BP, c])
        wait_bytes(part.vs[c].at[0:7], s.send_sem.at[BZ, c])


CHUNKED = dict(
    rcs=(NC, (128,), BF),
    rcr=(NC, (128,), BF),
    rmine=(NC, (128,), F32),
    rsum=(NC, (8, 16), BF),
    rrec=(NC, (8, 16), BF),
    zs=(NC + 1, (8, 16), BF),
    zr=(NC + 1, (8, 16), BF),
    ps=(NC + 1, (8, 16), BF),
    xin=(NC + 1, (2, 16, 16), BF),
    ycs=(NC, (256,), BF),
    ycr=(NC, (256,), BF),
    ymine=(NC, (256,), F32),
    ysum=(NC, (16, 16), BF),
    pr=(NC, (16, 16), BF),
    vs=(NC, (8, 16), BF),
    vr=(NC, (8, 16), BF),
)
SCRATCH = dict(
    hidden=pltpu.VMEM((D, 256), BF),
    w_in=pltpu.VMEM((160, D), BF),
    w_gain=pltpu.VMEM((160, D), BF),
    gain_in=pltpu.VMEM((D,), F32),
    keys=pltpu.VMEM((16, 128, 256), BF),
    values=pltpu.VMEM((16, 128, 256), BF),
    proj_out=pltpu.VMEM((16, 16, 256), BF),
    proj_in=pltpu.VMEM((8, 2, 16, 256), BF),
    spreading=pltpu.VMEM((320, 640), BF),
    heads=pltpu.VMEM((640, 128), F32),
    mixed=pltpu.VMEM((512, 128), F32),
    att_out=pltpu.VMEM((16, 16, 128), BF),
    att=pltpu.VMEM((8, 2, 16, 128), BF),
    own_hidden=pltpu.VMEM((16, D), F32),
    w_out=pltpu.VMEM((D, 128), BF),
    gain=pltpu.VMEM((D,), F32),
    index=pltpu.VMEM((4, 16), jnp.int32),
    share=pltpu.VMEM((4, 16), F32),
    gate=pltpu.VMEM((FFQ, D), BF),
    up=pltpu.VMEM((FFQ, D), BF),
    down=pltpu.VMEM((FFQ, D), BF),
    residual=pltpu.VMEM((16, D), F32),
    gate_out=pltpu.VMEM((512, FFQ), F32),
    up_out=pltpu.VMEM((512, FFQ), F32),
    active=pltpu.VMEM((512, FFQ), BF),
    load_sem=pltpu.SemaphoreType.DMA((12,)),
    send_sem=pltpu.SemaphoreType.DMA((10, NC + 1)),
    recv_sem=pltpu.SemaphoreType.DMA((10, NC + 1)),
)
PARTS = [
    pltpu.VMEM((*lead, WIDTHS[c]), dtype) for n, lead, dtype in CHUNKED.values() for c in range(n)
]


def per_device(
    hidden_rows,
    attention_gain,
    input_weight,
    cache_keys,
    cache_values,
    context_length,
    sink_logits,
    out_weight,
    expert_gain,
    expert_index,
    expert_share,
    gate_weight,
    up_weight,
    down_weight,
):
    scalars = pl.BlockSpec(memory_space=pltpu.SMEM)
    anywhere = pl.BlockSpec(memory_space=pltpu.HBM)
    return pl.pallas_call(
        layer,
        out_shape=jax.ShapeDtypeStruct((16, D), BF),
        in_specs=[scalars] * 2 + [anywhere] * 12,
        out_specs=pl.BlockSpec(memory_space=pltpu.VMEM),
        scratch_shapes=list(SCRATCH.values()) + PARTS,
        compiler_params=pltpu.CompilerParams(
            collective_id=0, has_side_effects=True, vmem_limit_bytes=60 * 1024 * 1024
        ),
        cost_estimate=pl.CostEstimate(
            flops=4_000_000_000, bytes_accessed=12_000_000, transcendentals=300_000
        ),
        name="layer",
    )(
        context_length,
        sink_logits,
        hidden_rows.T,
        input_weight.T,
        attention_gain,
        cache_keys,
        cache_values,
        out_weight.T,
        expert_gain,
        expert_index.T,
        expert_share.T,
        gate_weight,
        up_weight,
        down_weight,
    )


def solution(mesh):
    return jax.shard_map(
        per_device,
        mesh=mesh,
        in_specs=(
            P("attn", None),
            P(),
            P(None, "exp"),
            P(("attn", "exp"), None, None),
            P(("attn", "exp"), None, None),
            P(("attn", "exp")),
            P(),
            P("exp", None),
            P(),
            P(("attn", "exp"), None),
            P(("attn", "exp"), None),
            P(("attn", "exp"), None),
            P(("attn", "exp"), None),
            P(("attn", "exp"), None),
        ),
        out_specs=P(("attn", "exp"), None),
        check_vma=False,
    )
```
